128 devices in a mesh: stream: 4 (over y), azim: 8 (over x_lo, z), normal: 4 (over x_hi, core).
Axes of the slice: x: 4 (x_hi: 2, x_lo: 2; x = x_hi * 2 + x_lo), y: 4, z: 4, core: 2. Of those that a mesh axis runs over, the one named last changes fastest.
Arguments:
- perturbation: float32 [12, 32, 384, 1024], P(None, 'stream', 'normal', 'azim'), may hold values from -6 to 6
- base_flow: bfloat16 [8, 32, 384, 1024], P(None, 'stream', 'normal', 'azim'), may hold values from 0.25 to 2
- stream_ops: bfloat16 [2, 32, 32], replicated, may hold values from -1 to 1
- azimuth_ops: bfloat16 [2, 1024, 1024], replicated, may hold values from -0.1875 to 0.1875
- normal_ops: bfloat16 [2, 384, 384], replicated, may hold values from -0.3125 to 0.3125
- coupling: float32 [3, 12, 12], replicated, may hold values from -1.75 to 1.75
- chemistry: float32 [3, 12, 12], replicated, may hold values from -1.75 to 1.75
Outputs:
- advanced: float32 [12, 32, 384, 1024], P(None, 'stream', 'normal', 'azim')
The draws below stay inside these ranges and needn't reach their ends.
All inputs are finite; a program needn't handle non-finite values.
Results may differ from the reference program's by a relative error of at most 0.0019.
Values may be sent and summed in bfloat16 or wider, within the bound.
A program may use at most 256 MiB of HBM per device.

```python
import jax
import jax.numpy as jnp
from jax import lax

NV = 12
NB = 8
A = 1024
N = 384
S = 32


def block_scale(own_key, extent, shards, least, high):
    loudness, own = 1.0, jax.random.fold_in(own_key, 6)
    for axis_at, blocks in shards:
        steps = jnp.exp(jax.random.uniform(jax.random.fold_in(own, axis_at), (blocks,), jnp.float32, least / len(shards), high / len(shards)))
        loudness = loudness * jnp.repeat(steps, extent[axis_at] // blocks).reshape([-1 if axis == axis_at else 1 for axis in range(len(extent))])
    return loudness


def bell_draw(rng, extent, spread, bound, cuts=(), kind=jnp.bfloat16):
    factor_of = block_scale(rng, extent, cuts, -0.22, 0.18) if cuts else 1.0
    result = jax.random.normal(rng, extent, jnp.float32) * spread * factor_of
    return jnp.minimum(jnp.maximum(result, -bound), bound).astype(kind)


def setup_inputs(seed: int = 0) -> dict:
    splits = jax.random.split(jax.random.key(seed), 8)
    perturbation = bell_draw(splits[0], (NV, S, N, A), 1.0, 6.0, ((1, 4), (2, 4), (3, 8)), jnp.float32)
    base_flow = jnp.clip(0.25 + 1.75 * jax.random.uniform(splits[1], (NB, S, N, A), jnp.float32) ** block_scale(splits[1], (NB, S, N, A), ((1, 4), (2, 4), (3, 8)), -0.2, 0.2), 0.25, 2.0).astype(jnp.bfloat16)
    stream_ops = bell_draw(splits[2], (2, S, S), S ** -0.5, 1.0)
    azimuth_ops = bell_draw(splits[3], (2, A, A), A ** -0.5, 0.1875)
    normal_ops = bell_draw(splits[4], (2, N, N), N ** -0.5, 0.3125)
    coupling = bell_draw(splits[5], (3, NV, NV), NV ** -0.5, 1.75, (), jnp.float32)
    chemistry = bell_draw(splits[6], (3, NV, NV), NV ** -0.5, 1.75, (), jnp.float32)
    return {"perturbation": perturbation, "base_flow": base_flow, "stream_ops": stream_ops, "azimuth_ops": azimuth_ops, "normal_ops": normal_ops, "coupling": coupling, "chemistry": chemistry}


highest = lax.Precision.HIGHEST


def flux_terms(derivs, velocity, density, viscous, coupling_d):
    first_der = derivs[0]
    second_der = derivs[1]
    mixed = jnp.einsum("vw,wsna->vsna", coupling_d, first_der, precision=highest)
    return (-velocity.astype(jnp.float32) * first_der
            - density.astype(jnp.float32) * mixed
            + viscous.astype(jnp.float32) * second_der)


def reference(perturbation, base_flow, stream_ops, azimuth_ops, normal_ops, coupling, chemistry):
    lowered = perturbation.astype(jnp.bfloat16)
    wide = lowered.astype(jnp.float32)
    normal_der = jnp.einsum("kij,vsja->kvsia", normal_ops.astype(jnp.float32), wide, precision=highest)
    rate = flux_terms(normal_der, base_flow[2], base_flow[3], base_flow[4], coupling[2])
    normal_der = None
    azim_der = jnp.einsum("kij,vsnj->kvsni", azimuth_ops.astype(jnp.float32), wide, precision=highest)
    rate = rate + flux_terms(azim_der, base_flow[1], base_flow[3], base_flow[4], coupling[1])
    azim_der = None
    stream_der = jnp.einsum("kij,vjna->kvina", stream_ops.astype(jnp.float32), wide, precision=highest)
    rate = rate + flux_terms(stream_der, base_flow[0], base_flow[3], base_flow[4], coupling[0])
    stream_der = None
    parts = jnp.einsum("cvw,wsna->cvsna", chemistry, perturbation, precision=highest)
    source = (parts[0] + base_flow[5].astype(jnp.float32) * parts[1]
              + base_flow[6].astype(jnp.float32) * parts[2]
              - base_flow[7].astype(jnp.float32) * perturbation)
    rate = rate + source
    variable_ids = jnp.arange(NV, dtype=jnp.int32)
    wall_rows = jnp.arange(N, dtype=jnp.int32) == 0
    held = (variable_ids >= 5) & (variable_ids <= 9)
    pinned = held[:, None, None, None] & wall_rows[None, None, :, None]
    rate = jnp.where(pinned, jnp.float32(0.0), rate)
    return perturbation + 0.2 * rate
```

```python
import functools

import jax
import jax.numpy as jnp
from jax import lax
from jax.experimental import pallas as pl
from jax.experimental.pallas import tpu as pltpu
from jax.sharding import PartitionSpec as P

MESH = pl.DeviceIdType.MESH
F32, BF16 = jnp.float32, jnp.bfloat16
NV, S, N, A = 12, 8, 96, 128


def copies_table():
    table, count = {}, 0
    for t in range(2):
        for d in (1, 2, 3):
            for name in ("zf", "zb", "zr"):
                table[name, t, d] = count
                count += 1
        for d in range(4):
            for name in ("lo", "hi", "co", "cw"):
                table[name, t, d] = count
                count += 1
    for g in range(3):
        for d in (1, 2, 3):
            for name in ("yf", "yr"):
                table[name, g, d] = count
                count += 1
    return table, count


TABLE, COPIES = copies_table()


def spread(matrix, reps):
    rows, cols = matrix.shape
    shift = reps.bit_length() - 1
    up = (lax.broadcasted_iota(jnp.int32, (rows * reps, rows), 0) >> shift
          == lax.broadcasted_iota(jnp.int32, (rows * reps, rows), 1)).astype(F32).astype(BF16)
    wide = (lax.broadcasted_iota(jnp.int32, (cols, cols * reps), 1) >> shift
            == lax.broadcasted_iota(jnp.int32, (cols, cols * reps), 0)).astype(F32).astype(BF16)
    tall = jnp.dot(up, matrix, preferred_element_type=F32).astype(BF16)
    full = jnp.dot(tall, wide, preferred_element_type=F32)
    r = lax.broadcasted_iota(jnp.int32, full.shape, 0) & (reps - 1)
    c = lax.broadcasted_iota(jnp.int32, full.shape, 1) & (reps - 1)
    return jnp.where(r == c, full, 0.0).astype(BF16)


def split_two(matrix):
    high = matrix.astype(BF16)
    return high, (matrix - high.astype(F32)).astype(BF16)


def kernel(pert, base, sops, aops, nops, coup, chem, out,
           zs, zbs, gat, zbase, oth, ys, yr, fy, ry, fz, rz, dn, dy, wa, kc, ky, kz, ks, kn,
           ssem, rsem, lsem):
    y = lax.axis_index("stream")
    ai = lax.axis_index("azim")
    ni = lax.axis_index("normal")
    lo, z = ai // 4, ai % 4
    hi, core = ni // 2, ni % 2

    def at(y_=None, z_=None, lo_=None, hi_=None, core_=None):
        pick = lambda new, old: old if new is None else new
        return {"stream": pick(y_, y), "azim": pick(lo_, lo) * 4 + pick(z_, z),
                "normal": pick(hi_, hi) * 2 + pick(core_, core)}

    y_of = lambda d: (y + d) % 4
    z_of = lambda d: (z + d) % 4
    lo_dev = at(lo_=1 - lo)
    hi_dev = at(lo_=1 - lo, hi_=1 - hi)
    core_dev = at(core_=1 - core)
    slot_own = ni
    slot_core = hi * 2 + (1 - core)
    slot_hi = (1 - hi) * 2 + core
    slot_both = (1 - hi) * 2 + (1 - core)

    barrier = pltpu.get_barrier_semaphore()
    partners = [at(y_=y_of(d)) for d in (1, 2, 3)] + [at(z_=z_of(d)) for d in (1, 2, 3)] + [lo_dev, hi_dev, core_dev]
    for device in partners:
        pl.semaphore_signal(barrier, inc=1, device_id=device, device_id_type=MESH)

    def remote(src, dst, key, device):
        i = TABLE[key]
        return pltpu.make_async_remote_copy(src_ref=src, dst_ref=dst, send_sem=ssem.at[i], recv_sem=rsem.at[i],
                                            device_id=device, device_id_type=MESH)

    def zf(t, d):
        return remote(zs.at[2 * z_of(d) + t], gat.at[t, slot_own, z], ("zf", t, d), at(z_=z_of(d)))

    def zb(t, d):
        return remote(zbs.at[2 * z_of(d) + t], zbase.at[t, z], ("zb", t, d), at(z_=z_of(d)))

    def zr(t, d):
        return remote(fz.at[t, z_of(d)], rz.at[2 * z + t], ("zr", t, d), at(z_=z_of(d)))

    def src_own(t, d):
        return zs.at[2 * z + t] if d == 0 else gat.at[t, slot_own, z_of(-d)]

    def lo_c(t, d):
        return remote(src_own(t, d), oth.at[t, z_of(-d)], ("lo", t, d), lo_dev)

    def co(t, d):
        return remote(src_own(t, d), gat.at[t, slot_own, z_of(-d)], ("co", t, d), core_dev)

    def hi_c(t, d):
        return remote(oth.at[t, z_of(-d)], gat.at[t, slot_own, z_of(-d)], ("hi", t, d), hi_dev)

    def cw(t, d):
        return remote(gat.at[t, slot_hi, z_of(-d)], gat.at[t, slot_hi, z_of(-d)], ("cw", t, d), core_dev)

    def yf(g, d):
        return remote(ys.at[y_of(d) * 3 + g], yr.at[g, y], ("yf", g, d), at(y_=y_of(d)))

    def yret(g, d):
        return remote(fy.at[g, y_of(d)], ry.at[y * 3 + g], ("yr", g, d), at(y_=y_of(d)))

    weights = [
        pltpu.make_async_copy(aops.at[k, pl.ds(pl.multiple_of(lo * 512, 512), 512), pl.ds(pl.multiple_of(half * 512, 512), 512)],
                              wa.at[pl.ds(k * 512, 512), pl.ds(j * 512, 512)], lsem.at[2 * k + j])
        for k in range(2) for j, half in enumerate((lo, 1 - lo))
    ]
    for w in weights:
        w.start()

    def lower(st, _):
        zs[st] = pert[:, st].astype(BF16)
        for f in range(4):
            zbs[st, f] = base[1 + f, st]
        return 0

    lax.fori_loop(0, S, lower, 0)
    pl.semaphore_wait(barrier, len(partners))
    for d in (1, 3, 2):
        zf(0, d).start()
    for t in range(2):
        lo_c(t, 0).start()
        co(t, 0).start()
    own = []
    for t in range(2):
        own.append(pltpu.make_async_copy(zs.at[2 * z + t], gat.at[t, slot_own, z], lsem.at[4 + t]))
        own.append(pltpu.make_async_copy(zbs.at[2 * z + t], zbase.at[t, z], lsem.at[6 + t]))
    for c in own:
        c.start()

    def lower_y(i, _):
        rows = pert[:, :, pl.ds(pl.multiple_of(i * 8, 8), 8), :]
        ys[i, 0:NV] = rows.reshape(NV, 64, A).astype(BF16)
        return 0

    lax.fori_loop(0, 12, lower_y, 0)
    for j, f in enumerate((0, 3, 4)):
        wide = base[f].astype(F32)
        for i in range(12):
            ys[i, NV + j] = wide[:, 8 * i:8 * i + 8, :].reshape(64, A).astype(BF16)
    for g in range(3):
        for d in (1, 3, 2):
            yf(g, d).start()
    for d in (1, 3, 2):
        zb(0, d).start()
    for d in (1, 3, 2):
        zf(1, d).start()
    for d in (1, 3, 2):
        zb(1, d).start()
    yown = []
    for g in range(3):
        yown.append(pltpu.make_async_copy(ys.at[y * 3 + g], yr.at[g, y], lsem.at[8 + g]))
    for c in yown:
        c.start()

    ks[...] = spread(sops[...].reshape(64, 32), 8)
    c_high, c_low = split_two(coup[...])
    ky[:, 0:192] = spread(c_high[0], 16)
    ky[:, 192:384] = spread(c_low[0], 16)
    kz[:, 0:192] = spread(c_high[1], 16)
    kz[:, 192:384] = spread(c_high[2], 16)
    kz[:, 384:576] = spread(c_low[1], 16)
    kz[:, 576:768] = spread(c_low[2], 16)
    h_high, h_low = split_two(chem[...])
    for c in range(3):
        high = spread(h_high[c], 16)
        kc[192 * c:192 * c + 192, 0:192] = high
        kc[192 * c:192 * c + 192, 192:384] = high
        kc[192 * c:192 * c + 192, 384:576] = spread(h_low[c], 16)
    for k in range(2):
        kn[96 * k:96 * k + 96] = nops[k, pl.ds(pl.multiple_of(ni * 96, 96), 96), :]

    def scale_of(first_row, rows):
        row = lax.broadcasted_iota(jnp.int32, (rows, A), 0) + first_row + ni * N
        return jnp.where(row == 0, 0.0, 0.2).astype(F32)

    def source(st):
        def pair(q, _):
            r0 = pl.multiple_of(q * 32, 32)
            p = jnp.concatenate([pert[:, st, pl.ds(r0, 16), :].reshape(192, A),
                                 pert[:, st, pl.ds(pl.multiple_of(r0 + 16, 16), 16), :].reshape(192, A)], axis=1)
            high = p.astype(BF16)
            low = (p - high.astype(F32)).astype(BF16)
            parts = jnp.dot(kc[...], jnp.concatenate([high, low, high], axis=0), preferred_element_type=F32)
            parts = parts.reshape(3, NV, 16, 2 * A)
            p = p.reshape(NV, 16, 2 * A)
            for j in range(2):
                rj = pl.multiple_of(r0 + 16 * j, 16)
                lanes = slice(j * A, (j + 1) * A)
                b5, b6, b7 = (base[f, st, pl.ds(rj, 16), :].astype(F32) for f in (5, 6, 7))
                held = scale_of(rj, 16)
                for v in range(NV):
                    here = p[v, :, lanes]
                    src = parts[0, v, :, lanes] + b5 * parts[1, v, :, lanes] + b6 * parts[2, v, :, lanes] - b7 * here
                    out[v, st, pl.ds(rj, 16), :] = here + (held if 5 <= v <= 9 else 0.2) * src
            return 0
        lax.fori_loop(0, 3, pair, 0)

    def sources(first, count):
        def one(i, _):
            source(i)
            return 0
        lax.fori_loop(first, first + count, one, 0)

    def stream_flux(g):
        for d in (1, 3, 2):
            yf(g, d).wait_recv()
        yown[g].wait()

        def derive(q, _):
            x = jnp.concatenate([yr[g, :, 2 * q].reshape(256, A), yr[g, :, 2 * q + 1].reshape(256, A)], axis=1)
            both = jnp.dot(ks[...], x, preferred_element_type=F32)
            for j in range(2):
                dy[0, 2 * q + j] = both[0:256, j * A:(j + 1) * A]
                dy[1, 2 * q + j] = both[256:512, j * A:(j + 1) * A]
            return 0

        lax.fori_loop(0, NV // 2, derive, 0)

        def mix(q, _):
            dst, pr = q // 2, q % 2
            row = lambda j: pl.multiple_of(dst * 64 + pr * 32 + 16 * j, 16)
            first = jnp.concatenate([dy[0, :, pl.ds(row(j), 16), :].reshape(192, A) for j in range(2)], axis=1)
            low = first.astype(BF16)
            mixed = jnp.dot(ky[...], jnp.concatenate([low, low], axis=0), preferred_element_type=F32)
            mixed = mixed.reshape(NV, 16, 2 * A)
            for j in range(2):
                lanes = slice(j * A, (j + 1) * A)
                near = pl.multiple_of(pr * 32 + 16 * j, 16)
                u, rho, nu = (yr[g, dst, NV + f, pl.ds(near, 16), :].astype(F32) for f in range(3))
                for v in range(NV):
                    d1, d2 = dy[0, v, pl.ds(row(j), 16), :], dy[1, v, pl.ds(row(j), 16), :]
                    flux = nu * d2 - u * d1 - rho * mixed[v, :, lanes]
                    fy[g, dst, v, pl.ds(near, 16), :] = flux.astype(BF16)
            return 0

        lax.fori_loop(0, 8, mix, 0)
        for d in (1, 3, 2):
            yret(g, d).start()

    def turned_flux(t):
        def normal(v, _):
            x = jnp.concatenate([gat[t, :, b, v].reshape(384, A) for b in range(4)], axis=1)
            both = jnp.dot(kn[...], x, preferred_element_type=F32)
            dn[0, v] = both[0:96]
            dn[1, v] = both[96:192]
            return 0

        lax.fori_loop(0, NV, normal, 0)

        def rows_of(q, _):
            r = pl.ds(pl.multiple_of(q * 16, 16), 16)
            x = jnp.concatenate([gat[t, slot_own, b, :, r, :].reshape(192, A) for b in range(4)]
                                + [oth[t, b, :, r, :].reshape(192, A) for b in range(4)], axis=1)
            da = lax.dot_general(x, wa[...], (((1,), (1,)), ((), ())), preferred_element_type=F32)
            low_a = da[:, 0:512].astype(BF16)
            low_n = dn[0, :, r, :].reshape(192, 512).astype(BF16)
            mixed = jnp.dot(kz[...], jnp.concatenate([low_a, low_n, low_a, low_n], axis=0), preferred_element_type=F32)
            for b in range(4):
                lanes = slice(b * A, (b + 1) * A)
                u1, u2, rho, nu = (zbase[t, b, f, r, :].astype(F32) for f in range(4))
                for v in range(NV):
                    rv = slice(16 * v, 16 * v + 16)
                    a1, a2 = da[rv, lanes], da[rv, 512 + b * A:512 + (b + 1) * A]
                    n1, n2 = dn[0, v, r, lanes], dn[1, v, r, lanes]
                    flux = nu * (a2 + n2) - u1 * a1 - u2 * n1 - rho * mixed[rv, lanes]
                    fz[t, b, v, r, :] = flux.astype(BF16)
            return 0

        lax.fori_loop(0, N // 16, rows_of, 0)
        for d in (1, 3, 2):
            zr(t, d).start()

    def pass_lo(t, d):
        zf(t, d).wait_recv()
        lo_c(t, d).start()
        co(t, d).start()

    def pass_hi(t, d):
        lo_c(t, d).wait_recv()
        hi_c(t, d).start()

    def pass_core(t, d):
        hi_c(t, d).wait_recv()
        cw(t, d).start()

    def wait_station(t):
        for d in range(4):
            co(t, d).wait_recv()
            cw(t, d).wait_recv()
        for d in (1, 2, 3):
            zb(t, d).wait_recv()
        own[2 * t].wait()
        own[2 * t + 1].wait()

    def add_stream(g, d):
        i = y_of(-d) * 3 + g
        r = pl.ds(pl.multiple_of(i * 8, 8), 8)
        held = scale_of(i * 8, 8)
        for v in range(NV):
            src = fy[g, y, v] if d == 0 else ry[i, v]
            out[v, :, r, :] += (held if 5 <= v <= 9 else 0.2) * src.astype(F32).reshape(S, 8, A)

    def add_turned(t, d):
        st = 2 * z_of(-d) + t
        held = scale_of(0, N)
        for v in range(NV):
            src = fz[t, z, v] if d == 0 else rz[st, v]
            out[v, st] += (held if 5 <= v <= 9 else 0.2) * src.astype(F32)

    sources(0, 2)
    pass_hi(0, 0)
    sources(2, 1)
    pass_lo(0, 1)
    pass_lo(0, 3)
    stream_flux(0)
    pass_hi(1, 0)
    pass_core(0, 0)
    sources(3, 1)
    pass_lo(0, 2)
    pass_hi(0, 1)
    pass_core(1, 0)
    stream_flux(1)
    pass_hi(0, 3)
    pass_core(0, 1)
    sources(4, 1)
    pass_lo(1, 1)
    pass_lo(1, 3)
    pass_hi(0, 2)
    pass_core(0, 3)
    stream_flux(2)
    pass_lo(1, 2)
    sources(5, 3)
    pass_hi(1, 1)
    pass_core(0, 2)
    for w in weights:
        w.wait()
    wait_station(0)
    turned_flux(0)
    pass_hi(1, 3)
    pass_core(1, 1)
    for g in range(2):
        add_stream(g, 0)
        for d in (1, 3, 2):
            yret(g, d).wait_recv()
            add_stream(g, d)
    pass_hi(1, 2)
    pass_core(1, 3)
    add_stream(2, 0)
    for d in (1, 3, 2):
        yret(2, d).wait_recv()
        add_stream(2, d)
    pass_core(1, 2)
    wait_station(1)
    turned_flux(1)
    for t in range(2):
        add_turned(t, 0)
        for d in (1, 3, 2):
            zr(t, d).wait_recv()
            add_turned(t, d)
    for t in range(2):
        for d in range(4):
            for copy in (lo_c, co, hi_c, cw):
                copy(t, d).wait_send()
        for d in (1, 2, 3):
            for copy in (zf, zb, zr):
                copy(t, d).wait_send()
    for g in range(3):
        for d in (1, 2, 3):
            yf(g, d).wait_send()
            yret(g, d).wait_send()


def shards(perturbation, base_flow, stream_ops, azimuth_ops, normal_ops, coupling, chemistry):
    vmem = pl.BlockSpec(memory_space=pltpu.VMEM)
    scratch = lambda *shape: pltpu.VMEM(shape, BF16)
    return pl.pallas_call(
        kernel,
        out_shape=jax.ShapeDtypeStruct(perturbation.shape, F32),
        in_specs=[vmem, vmem, vmem, pl.BlockSpec(memory_space=pl.ANY), vmem, vmem, vmem],
        out_specs=vmem,
        scratch_shapes=[
            scratch(S, NV, N, A),
            scratch(S, 4, N, A),
            scratch(2, 4, 4, NV, N, A),
            scratch(2, 4, 4, N, A),
            scratch(2, 4, NV, N, A),
            scratch(12, 15, 64, A),
            scratch(3, 4, 15, 64, A),
            scratch(3, 4, NV, 64, A),
            scratch(12, NV, 64, A),
            scratch(2, 4, NV, N, A),
            scratch(S, NV, N, A),
            pltpu.VMEM((2, NV, N, 512), F32),
            pltpu.VMEM((2, NV, 256, A), F32),
            scratch(1024, 1024),
            scratch(576, 576),
            scratch(192, 384),
            scratch(192, 768),
            scratch(512, 256),
            scratch(192, 384),
            pltpu.SemaphoreType.DMA((COPIES,)),
            pltpu.SemaphoreType.DMA((COPIES,)),
            pltpu.SemaphoreType.DMA((11,)),
        ],
        compiler_params=pltpu.CompilerParams(collective_id=0, has_side_effects=True, vmem_limit_bytes=62 << 20),
    )(perturbation, base_flow, stream_ops, azimuth_ops, normal_ops, coupling, chemistry)


def solution(mesh):
    field = P(None, "stream", "normal", "azim")
    return jax.shard_map(
        shards,
        mesh=mesh,
        in_specs=(field, field, P(), P(), P(), P(), P()),
        out_specs=field,
        check_vma=False,
    )
```

```python
import functools

import jax
import jax.numpy as jnp
from jax import lax
from jax.experimental import pallas as pl
from jax.experimental.pallas import tpu as pltpu
from jax.sharding import PartitionSpec as P

MESH = pl.DeviceIdType.MESH
F32, BF16 = jnp.float32, jnp.bfloat16
NV, S, N, A = 12, 8, 96, 128


def copies_table():
    table, count = {}, 0
    for t in range(2):
        for d in (1, 2, 3):
            for name in ("zf", "zb", "zr"):
                table[name, t, d] = count
                count += 1
        for d in range(4):
            for name in ("lo", "hi", "co", "cw"):
                table[name, t, d] = count
                count += 1
    for g in range(3):
        for d in (1, 2, 3):
            for name in ("yf", "yr"):
                table[name, g, d] = count
                count += 1
    return table, count


TABLE, COPIES = copies_table()


def spread(matrix, reps):
    rows, cols = matrix.shape
    shift = reps.bit_length() - 1
    up = (lax.broadcasted_iota(jnp.int32, (rows * reps, rows), 0) >> shift
          == lax.broadcasted_iota(jnp.int32, (rows * reps, rows), 1)).astype(F32).astype(BF16)
    wide = (lax.broadcasted_iota(jnp.int32, (cols, cols * reps), 1) >> shift
            == lax.broadcasted_iota(jnp.int32, (cols, cols * reps), 0)).astype(F32).astype(BF16)
    tall = jnp.dot(up, matrix, preferred_element_type=F32).astype(BF16)
    full = jnp.dot(tall, wide, preferred_element_type=F32)
    r = lax.broadcasted_iota(jnp.int32, full.shape, 0) & (reps - 1)
    c = lax.broadcasted_iota(jnp.int32, full.shape, 1) & (reps - 1)
    return jnp.where(r == c, full, 0.0).astype(BF16)


def split_two(matrix):
    high = matrix.astype(BF16)
    return high, (matrix - high.astype(F32)).astype(BF16)


def kernel(pert_hbm, base_hbm, sops, aops, nops, coup, chem, out_hbm,
           pert, base, out, zs, zbs, gat, zbase, oth, ys, yr, fy, ry, fz, rz, da, dn, dy, wa, kc, ky, kz, ks, kn,
           ssem, rsem, lsem, isem, wsem, osem):
    loads = [(pltpu.make_async_copy(pert_hbm.at[:, st], pert.at[:, st], isem.at[2 * st]),
              pltpu.make_async_copy(base_hbm.at[:, st], base.at[:, st], isem.at[2 * st + 1])) for st in range(S)]
    for pair in loads:
        for load in pair:
            load.start()
    y = lax.axis_index("stream")
    ai = lax.axis_index("azim")
    ni = lax.axis_index("normal")
    lo, z = ai // 4, ai % 4
    hi, core = ni // 2, ni % 2

    def at(y_=None, z_=None, lo_=None, hi_=None, core_=None):
        pick = lambda new, old: old if new is None else new
        return {"stream": pick(y_, y), "azim": pick(lo_, lo) * 4 + pick(z_, z),
                "normal": pick(hi_, hi) * 2 + pick(core_, core)}

    y_of = lambda d: (y + d) % 4
    z_of = lambda d: (z + d) % 4
    lo_dev = at(lo_=1 - lo)
    hi_dev = at(lo_=1 - lo, hi_=1 - hi)
    core_dev = at(core_=1 - core)
    slot_own = ni
    slot_core = hi * 2 + (1 - core)
    slot_hi = (1 - hi) * 2 + core
    slot_both = (1 - hi) * 2 + (1 - core)

    barrier = pltpu.get_barrier_semaphore()
    partners = [at(y_=y_of(d)) for d in (1, 2, 3)] + [at(z_=z_of(d)) for d in (1, 2, 3)] + [lo_dev, hi_dev, core_dev]
    for device in partners:
        pl.semaphore_signal(barrier, inc=1, device_id=device, device_id_type=MESH)

    def remote(src, dst, key, device):
        i = TABLE[key]
        return pltpu.make_async_remote_copy(src_ref=src, dst_ref=dst, send_sem=ssem.at[i], recv_sem=rsem.at[i],
                                            device_id=device, device_id_type=MESH)

    def zf(t, d):
        return remote(zs.at[2 * z_of(d) + t], gat.at[t, slot_own, z], ("zf", t, d), at(z_=z_of(d)))

    def zb(t, d):
        return remote(zbs.at[2 * z_of(d) + t], zbase.at[t, z], ("zb", t, d), at(z_=z_of(d)))

    def zr(t, d):
        return remote(fz.at[t, z_of(d)], rz.at[2 * z + t], ("zr", t, d), at(z_=z_of(d)))

    def src_own(t, d):
        return zs.at[2 * z + t] if d == 0 else gat.at[t, slot_own, z_of(-d)]

    def lo_c(t, d):
        return remote(src_own(t, d), oth.at[t, z_of(-d)], ("lo", t, d), lo_dev)

    def co(t, d):
        return remote(src_own(t, d), gat.at[t, slot_own, z_of(-d)], ("co", t, d), core_dev)

    def hi_c(t, d):
        return remote(oth.at[t, z_of(-d)], gat.at[t, slot_own, z_of(-d)], ("hi", t, d), hi_dev)

    def cw(t, d):
        return remote(gat.at[t, slot_hi, z_of(-d)], gat.at[t, slot_hi, z_of(-d)], ("cw", t, d), core_dev)

    def yf(g, d):
        return remote(ys.at[y_of(d) * 3 + g], yr.at[g, y], ("yf", g, d), at(y_=y_of(d)))

    def yret(g, d):
        return remote(fy.at[g, y_of(d)], ry.at[y * 3 + g], ("yr", g, d), at(y_=y_of(d)))

    for st in range(S):
        for load in loads[st]:
            load.wait()
        zs[st] = pert[:, st].astype(BF16)
        for f in range(4):
            zbs[st, f] = base[1 + f, st]
    pl.semaphore_wait(barrier, len(partners))
    for d in (1, 3, 2):
        zf(0, d).start()
    for t in range(2):
        lo_c(t, 0).start()
        co(t, 0).start()
    own = []
    for t in range(2):
        own.append(pltpu.make_async_copy(zs.at[2 * z + t], gat.at[t, slot_own, z], lsem.at[4 + t]))
        own.append(pltpu.make_async_copy(zbs.at[2 * z + t], zbase.at[t, z], lsem.at[6 + t]))
    for c in own:
        c.start()

    def lower_y(i, _):
        rows = pert[:, :, pl.ds(pl.multiple_of(i * 8, 8), 8), :]
        ys[i, 0:NV] = rows.reshape(NV, 64, A).astype(BF16)
        return 0

    lax.fori_loop(0, 12, lower_y, 0)
    for j, f in enumerate((0, 3, 4)):
        wide = base[f].astype(F32)
        for i in range(12):
            ys[i, NV + j] = wide[:, 8 * i:8 * i + 8, :].reshape(64, A).astype(BF16)
    for g in range(3):
        for d in (1, 3, 2):
            yf(g, d).start()
    for d in (1, 3, 2):
        zb(0, d).start()
    for d in (1, 3, 2):
        zf(1, d).start()
    for d in (1, 3, 2):
        zb(1, d).start()
    yown = []
    for g in range(3):
        yown.append(pltpu.make_async_copy(ys.at[y * 3 + g], yr.at[g, y], lsem.at[8 + g]))
    for c in yown:
        c.start()
    weights = [
        pltpu.make_async_copy(
            aops.at[k, pl.ds(pl.multiple_of(lo * 512, 512), 512), pl.ds(pl.multiple_of(half * 512 + b * A, A), A)],
            wa.at[j, b, pl.ds(k * 512, 512)], wsem.at[8 * k + 4 * j + b])
        for k in range(2) for j, half in enumerate((lo, 1 - lo)) for b in range(4)
    ]
    for w in weights:
        w.start()

    ks[...] = spread(sops[...].reshape(64, 32), 8)
    c_high, c_low = split_two(coup[...])
    ky[:, 0:192] = spread(c_high[0], 16)
    ky[:, 192:384] = spread(c_low[0], 16)
    kz[:, 0:192] = spread(c_high[1], 16)
    kz[:, 192:384] = spread(c_high[2], 16)
    kz[:, 384:576] = spread(c_low[1], 16)
    kz[:, 576:768] = spread(c_low[2], 16)
    h_high, h_low = split_two(chem[...])
    for c in range(3):
        high = spread(h_high[c], 16)
        kc[192 * c:192 * c + 192, 0:192] = high
        kc[192 * c:192 * c + 192, 192:384] = high
        kc[192 * c:192 * c + 192, 384:576] = spread(h_low[c], 16)
    for k in range(2):
        kn[96 * k:96 * k + 96] = nops[k, pl.ds(pl.multiple_of(ni * 96, 96), 96), :]

    def scale_of(first_row, rows):
        row = lax.broadcasted_iota(jnp.int32, (rows, A), 0) + first_row + ni * N
        return jnp.where(row == 0, 0.0, 0.2).astype(F32)

    def source(st):
        def pair(q, _):
            r0 = pl.multiple_of(q * 32, 32)
            p = jnp.concatenate([pert[:, st, pl.ds(r0, 16), :].reshape(192, A),
                                 pert[:, st, pl.ds(pl.multiple_of(r0 + 16, 16), 16), :].reshape(192, A)], axis=1)
            high = p.astype(BF16)
            low = (p - high.astype(F32)).astype(BF16)
            parts = jnp.dot(kc[...], jnp.concatenate([high, low, high], axis=0), preferred_element_type=F32)
            parts = parts.reshape(3, NV, 16, 2 * A)
            p = p.reshape(NV, 16, 2 * A)
            for j in range(2):
                rj = pl.multiple_of(r0 + 16 * j, 16)
                lanes = slice(j * A, (j + 1) * A)
                b5, b6, b7 = (base[f, st, pl.ds(rj, 16), :].astype(F32) for f in (5, 6, 7))
                held = scale_of(rj, 16)
                for v in range(NV):
                    here = p[v, :, lanes]
                    src = parts[0, v, :, lanes] + b5 * parts[1, v, :, lanes] + b6 * parts[2, v, :, lanes] - b7 * here
                    out[v, st, pl.ds(rj, 16), :] = here + (held if 5 <= v <= 9 else 0.2) * src
            return 0
        lax.fori_loop(0, 3, pair, 0)

    def sources(first, count):
        def one(i, _):
            source(i)
            return 0
        lax.fori_loop(first, first + count, one, 0)

    def stream_flux(g):
        for d in (1, 3, 2):
            yf(g, d).wait_recv()
        yown[g].wait()

        def derive(q, _):
            x = jnp.concatenate([yr[g, :, 2 * q].reshape(256, A), yr[g, :, 2 * q + 1].reshape(256, A)], axis=1)
            both = jnp.dot(ks[...], x, preferred_element_type=F32)
            for j in range(2):
                dy[0, 2 * q + j] = both[0:256, j * A:(j + 1) * A]
                dy[1, 2 * q + j] = both[256:512, j * A:(j + 1) * A]
            return 0

        lax.fori_loop(0, NV // 2, derive, 0)

        def mix(q, _):
            dst, pr = q // 2, q % 2
            row = lambda j: pl.multiple_of(dst * 64 + pr * 32 + 16 * j, 16)
            first = jnp.concatenate([dy[0, :, pl.ds(row(j), 16), :].reshape(192, A) for j in range(2)], axis=1)
            low = first.astype(BF16)
            mixed = jnp.dot(ky[...], jnp.concatenate([low, low], axis=0), preferred_element_type=F32)
            mixed = mixed.reshape(NV, 16, 2 * A)
            for j in range(2):
                lanes = slice(j * A, (j + 1) * A)
                near = pl.multiple_of(pr * 32 + 16 * j, 16)
                u, rho, nu = (yr[g, dst, NV + f, pl.ds(near, 16), :].astype(F32) for f in range(3))
                for v in range(NV):
                    d1, d2 = dy[0, v, pl.ds(row(j), 16), :], dy[1, v, pl.ds(row(j), 16), :]
                    flux = nu * d2 - u * d1 - rho * mixed[v, :, lanes]
                    fy[g, dst, v, pl.ds(near, 16), :] = flux.astype(BF16)
            return 0

        lax.fori_loop(0, 8, mix, 0)
        for d in (1, 3, 2):
            yret(g, d).start()

    def azimuth(t, own_blocks, other_blocks, fresh):
        def rows_of(q, _):
            r = pl.ds(pl.multiple_of(q * 16, 16), 16)
            x = [gat[t, slot_own, b, :, r, :].reshape(192, A) for b in own_blocks]
            x += [oth[t, b, :, r, :].reshape(192, A) for b in other_blocks]
            w = [wa[0, b] for b in own_blocks] + [wa[1, b] for b in other_blocks]
            both = lax.dot_general(jnp.concatenate(x, axis=1), jnp.concatenate(w, axis=1), (((1,), (1,)), ((), ())),
                                   preferred_element_type=F32)
            for k in range(2):
                for b in range(4):
                    part = both[:, k * 512 + b * A:k * 512 + (b + 1) * A].reshape(NV, 16, A)
                    if not fresh:
                        part = part + da[k, b, :, r, :]
                    da[k, b, :, r, :] = part
            return 0

        lax.fori_loop(0, N // 16, rows_of, 0)

    def turned_flux(t, d):
        b = z_of(-d)
        co(t, d).wait_recv()
        cw(t, d).wait_recv()
        if d:
            zb(t, d).wait_recv()

        def normal(q, _):
            x = jnp.concatenate([gat[t, :, b, 2 * q].reshape(384, A), gat[t, :, b, 2 * q + 1].reshape(384, A)], axis=1)
            both = jnp.dot(kn[...], x, preferred_element_type=F32)
            for j in range(2):
                for k in range(2):
                    dn[k, 2 * q + j] = both[96 * k:96 * k + 96, j * A:(j + 1) * A]
            return 0

        lax.fori_loop(0, NV // 2, normal, 0)

        def mix(q, _):
            rs = [pl.ds(pl.multiple_of(q * 32 + 16 * j, 16), 16) for j in range(2)]
            low_a = jnp.concatenate([da[0, b, :, r, :].reshape(192, A) for r in rs], axis=1).astype(BF16)
            low_n = jnp.concatenate([dn[0, :, r, :].reshape(192, A) for r in rs], axis=1).astype(BF16)
            mixed = jnp.dot(kz[...], jnp.concatenate([low_a, low_n, low_a, low_n], axis=0), preferred_element_type=F32)
            for j, r in enumerate(rs):
                lanes = slice(j * A, (j + 1) * A)
                u1, u2, rho, nu = (zbase[t, b, f, r, :].astype(F32) for f in range(4))
                for v in range(NV):
                    flux = (nu * (da[1, b, v, r, :] + dn[1, v, r, :]) - u1 * da[0, b, v, r, :] - u2 * dn[0, v, r, :]
                            - rho * mixed[16 * v:16 * v + 16, lanes])
                    fz[t, b, v, r, :] = flux.astype(BF16)
            return 0

        lax.fori_loop(0, N // 32, mix, 0)
        if d:
            zr(t, 4 - d).start()

    def pass_lo(t, d):
        zf(t, d).wait_recv()
        lo_c(t, d).start()
        co(t, d).start()

    def pass_hi(t, d):
        lo_c(t, d).wait_recv()
        hi_c(t, d).start()

    def pass_core(t, d):
        hi_c(t, d).wait_recv()
        cw(t, d).start()

    def add_stream(g, d):
        i = y_of(-d) * 3 + g
        r = pl.ds(pl.multiple_of(i * 8, 8), 8)
        held = scale_of(i * 8, 8)
        for v in range(NV):
            src = fy[g, y, v] if d == 0 else ry[i, v]
            out[v, :, r, :] += (held if 5 <= v <= 9 else 0.2) * src.astype(F32).reshape(S, 8, A)

    def add_turned(t, d):
        st = 2 * z_of(-d) + t
        held = scale_of(0, N)
        for v in range(NV):
            src = fz[t, z, v] if d == 0 else rz[st, v]
            out[v, st] += (held if 5 <= v <= 9 else 0.2) * src.astype(F32)
        store(t, d).start()

    def store(t, d):
        st = 2 * z_of(-d) + t
        return pltpu.make_async_copy(out.at[:, st], out_hbm.at[:, st], osem.at[4 * t + d])

    sources(0, 2)
    pass_hi(0, 0)
    sources(2, 1)
    pass_lo(0, 1)
    pass_lo(0, 3)
    sources(3, 1)
    pass_hi(1, 0)
    pass_core(0, 0)
    sources(4, 1)
    pass_lo(0, 2)
    sources(5, 1)
    pass_hi(0, 1)
    pass_core(1, 0)
    stream_flux(0)
    sources(6, 1)
    pass_hi(0, 3)
    pass_core(0, 1)
    sources(7, 1)
    pass_lo(1, 1)
    pass_lo(1, 3)
    for w in weights:
        w.wait()
    for c in own:
        c.wait()
    pass_hi(0, 2)
    pass_core(0, 3)
    pass_lo(1, 2)
    azimuth(0, range(4), range(4), True)
    stream_flux(1)
    pass_hi(1, 1)
    pass_core(0, 2)
    for d in (1, 3, 0):
        turned_flux(0, d)
    stream_flux(2)
    turned_flux(0, 2)
    pass_hi(1, 3)
    pass_core(1, 1)
    azimuth(1, range(4), [z_of(-d) for d in (0, 1, 3)], True)
    add_stream(0, 0)
    pass_hi(1, 2)
    pass_core(1, 3)
    azimuth(1, [], [z_of(-2)], False)
    turned_flux(1, 1)
    turned_flux(1, 3)
    pass_core(1, 2)
    turned_flux(1, 2)
    turned_flux(1, 0)
    for g in range(3):
        if g:
            add_stream(g, 0)
        for d in (1, 3, 2):
            yret(g, d).wait_recv()
            add_stream(g, d)
    for t in range(2):
        for d in (0, 1, 3, 2):
            if d:
                zr(t, d).wait_recv()
            add_turned(t, d)
    for t in range(2):
        for d in range(4):
            store(t, d).wait()
    for t in range(2):
        for d in range(4):
            for copy in (lo_c, co, hi_c, cw):
                copy(t, d).wait_send()
        for d in (1, 2, 3):
            for copy in (zf, zb, zr):
                copy(t, d).wait_send()
    for g in range(3):
        for d in (1, 2, 3):
            yf(g, d).wait_send()
            yret(g, d).wait_send()


def shards(perturbation, base_flow, stream_ops, azimuth_ops, normal_ops, coupling, chemistry):
    vmem = pl.BlockSpec(memory_space=pltpu.VMEM)
    hbm = pl.BlockSpec(memory_space=pl.ANY)
    scratch = lambda *shape: pltpu.VMEM(shape, BF16)
    return pl.pallas_call(
        kernel,
        out_shape=jax.ShapeDtypeStruct(perturbation.shape, F32),
        in_specs=[hbm, hbm, vmem, hbm, vmem, vmem, vmem],
        out_specs=hbm,
        scratch_shapes=[
            pltpu.VMEM((NV, S, N, A), F32),
            scratch(8, S, N, A),
            pltpu.VMEM((NV, S, N, A), F32),
            scratch(S, NV, N, A),
            scratch(S, 4, N, A),
            scratch(2, 4, 4, NV, N, A),
            scratch(2, 4, 4, N, A),
            scratch(2, 4, NV, N, A),
            scratch(12, 15, 64, A),
            scratch(3, 4, 15, 64, A),
            scratch(3, 4, NV, 64, A),
            scratch(12, NV, 64, A),
            scratch(2, 4, NV, N, A),
            scratch(S, NV, N, A),
            pltpu.VMEM((2, 4, NV, N, A), F32),
            pltpu.VMEM((2, NV, N, A), F32),
            pltpu.VMEM((2, NV, 256, A), F32),
            scratch(2, 4, 1024, A),
            scratch(576, 576),
            scratch(192, 384),
            scratch(192, 768),
            scratch(512, 256),
            scratch(192, 384),
            pltpu.SemaphoreType.DMA((COPIES,)),
            pltpu.SemaphoreType.DMA((COPIES,)),
            pltpu.SemaphoreType.DMA((11,)),
            pltpu.SemaphoreType.DMA((2 * S,)),
            pltpu.SemaphoreType.DMA((16,)),
            pltpu.SemaphoreType.DMA((8,)),
        ],
        compiler_params=pltpu.CompilerParams(collective_id=0, has_side_effects=True, vmem_limit_bytes=62 << 20),
    )(perturbation, base_flow, stream_ops, azimuth_ops, normal_ops, coupling, chemistry)


def solution(mesh):
    field = P(None, "stream", "normal", "azim")
    return jax.shard_map(
        shards,
        mesh=mesh,
        in_specs=(field, field, P(), P(), P(), P(), P()),
        out_specs=field,
        check_vma=False,
    )
```

```python
import functools

import jax
import jax.numpy as jnp
from jax import lax
from jax.experimental import pallas as pl
from jax.experimental.pallas import tpu as pltpu
from jax.sharding import PartitionSpec as P

MESH = pl.DeviceIdType.MESH
F32, BF16 = jnp.float32, jnp.bfloat16
NV, S, N, A = 12, 8, 96, 128


def copies_table():
    table, count = {}, 0
    for t in range(2):
        for d in (1, 2, 3):
            for name in ("zf", "zb", "zr"):
                table[name, t, d] = count
                count += 1
        for d in range(4):
            for name in ("lo", "hi", "co", "cw"):
                table[name, t, d] = count
                count += 1
    for g in range(3):
        for d in (1, 2, 3):
            for name in ("yf", "yr"):
                table[name, g, d] = count
                count += 1
    return table, count


TABLE, COPIES = copies_table()


def spread(matrix, reps):
    rows, cols = matrix.shape
    shift = reps.bit_length() - 1
    up = (lax.broadcasted_iota(jnp.int32, (rows * reps, rows), 0) >> shift
          == lax.broadcasted_iota(jnp.int32, (rows * reps, rows), 1)).astype(F32).astype(BF16)
    wide = (lax.broadcasted_iota(jnp.int32, (cols, cols * reps), 1) >> shift
            == lax.broadcasted_iota(jnp.int32, (cols, cols * reps), 0)).astype(F32).astype(BF16)
    tall = jnp.dot(up, matrix, preferred_element_type=F32).astype(BF16)
    full = jnp.dot(tall, wide, preferred_element_type=F32)
    r = lax.broadcasted_iota(jnp.int32, full.shape, 0) & (reps - 1)
    c = lax.broadcasted_iota(jnp.int32, full.shape, 1) & (reps - 1)
    return jnp.where(r == c, full, 0.0).astype(BF16)


def split_two(matrix):
    high = matrix.astype(BF16)
    return high, (matrix - high.astype(F32)).astype(BF16)


def kernel(pert_hbm, base_hbm, sops, aops, nops, coup, chem, out,
           pert, base, zs, zbs, gat, zbase, oth, ys, yr, fy, ry, fz, rz, da, dn, dy, wa, kc, ky, kz, ks, kn,
           ssem, rsem, lsem, isem, wsem):
    y = lax.axis_index("stream")
    ai = lax.axis_index("azim")
    ni = lax.axis_index("normal")
    lo, z = ai // 4, ai % 4
    hi, core = ni // 2, ni % 2

    def at(y_=None, z_=None, lo_=None, hi_=None, core_=None):
        pick = lambda new, old: old if new is None else new
        return {"stream": pick(y_, y), "azim": pick(lo_, lo) * 4 + pick(z_, z),
                "normal": pick(hi_, hi) * 2 + pick(core_, core)}

    y_of = lambda d: (y + d) % 4
    z_of = lambda d: (z + d) % 4
    lo_dev = at(lo_=1 - lo)
    hi_dev = at(lo_=1 - lo, hi_=1 - hi)
    core_dev = at(core_=1 - core)
    slot_own = ni
    slot_core = hi * 2 + (1 - core)
    slot_hi = (1 - hi) * 2 + core
    slot_both = (1 - hi) * 2 + (1 - core)

    stations = [2 * z_of(d) + t for t in range(2) for d in (0, 1, 3, 2)]
    loads = [(pltpu.make_async_copy(pert_hbm.at[:, st], pert.at[:, st], isem.at[2 * i]),
              pltpu.make_async_copy(base_hbm.at[:, st], base.at[:, st], isem.at[2 * i + 1]))
             for i, st in enumerate(stations)]
    for pair in loads:
        for load in pair:
            load.start()
    barrier = pltpu.get_barrier_semaphore()
    partners = [at(y_=y_of(d)) for d in (1, 2, 3)] + [at(z_=z_of(d)) for d in (1, 2, 3)] + [lo_dev, hi_dev, core_dev]
    for device in partners:
        pl.semaphore_signal(barrier, inc=1, device_id=device, device_id_type=MESH)

    def remote(src, dst, key, device):
        i = TABLE[key]
        return pltpu.make_async_remote_copy(src_ref=src, dst_ref=dst, send_sem=ssem.at[i], recv_sem=rsem.at[i],
                                            device_id=device, device_id_type=MESH)

    def zf(t, d):
        return remote(zs.at[2 * z_of(d) + t], gat.at[t, slot_own, z], ("zf", t, d), at(z_=z_of(d)))

    def zb(t, d):
        return remote(zbs.at[2 * z_of(d) + t], zbase.at[t, z], ("zb", t, d), at(z_=z_of(d)))

    def zr(t, d):
        return remote(fz.at[t, z_of(d)], rz.at[2 * z + t], ("zr", t, d), at(z_=z_of(d)))

    def src_own(t, d):
        return zs.at[2 * z + t] if d == 0 else gat.at[t, slot_own, z_of(-d)]

    def lo_c(t, d):
        return remote(src_own(t, d), oth.at[t, z_of(-d)], ("lo", t, d), lo_dev)

    def co(t, d):
        return remote(src_own(t, d), gat.at[t, slot_own, z_of(-d)], ("co", t, d), core_dev)

    def hi_c(t, d):
        return remote(oth.at[t, z_of(-d)], gat.at[t, slot_own, z_of(-d)], ("hi", t, d), hi_dev)

    def cw(t, d):
        return remote(gat.at[t, slot_hi, z_of(-d)], gat.at[t, slot_hi, z_of(-d)], ("cw", t, d), core_dev)

    def yf(g, d):
        return remote(ys.at[y_of(d) * 3 + g], yr.at[g, y], ("yf", g, d), at(y_=y_of(d)))

    def yret(g, d):
        return remote(fy.at[g, y_of(d)], ry.at[y * 3 + g], ("yr", g, d), at(y_=y_of(d)))

    def lower(i):
        for load in loads[i]:
            load.wait()
        st = stations[i]
        zs[st] = pert[:, st].astype(BF16)
        for f in range(4):
            zbs[st, f] = base[1 + f, st]

    lower(0)
    pl.semaphore_wait(barrier, len(partners))
    lo_c(0, 0).start()
    co(0, 0).start()
    for i, d in enumerate((1, 3, 2)):
        lower(1 + i)
        zf(0, d).start()
    lower(4)
    lo_c(1, 0).start()
    co(1, 0).start()
    for i in (5, 6, 7):
        lower(i)
    own = []
    for t in range(2):
        own.append(pltpu.make_async_copy(zs.at[2 * z + t], gat.at[t, slot_own, z], lsem.at[4 + t]))
        own.append(pltpu.make_async_copy(zbs.at[2 * z + t], zbase.at[t, z], lsem.at[6 + t]))
    for c in own:
        c.start()

    def lower_y(i, _):
        rows = pert[:, :, pl.ds(pl.multiple_of(i * 8, 8), 8), :]
        ys[i, 0:NV] = rows.reshape(NV, 64, A).astype(BF16)
        return 0

    lax.fori_loop(0, 12, lower_y, 0)
    for j, f in enumerate((0, 3, 4)):
        wide = base[f].astype(F32)
        for i in range(12):
            ys[i, NV + j] = wide[:, 8 * i:8 * i + 8, :].reshape(64, A).astype(BF16)
    for g in range(3):
        for d in (1, 3, 2):
            yf(g, d).start()
    for d in (1, 3, 2):
        zb(0, d).start()
    for d in (1, 3, 2):
        zf(1, d).start()
    for d in (1, 3, 2):
        zb(1, d).start()
    yown = []
    for g in range(3):
        yown.append(pltpu.make_async_copy(ys.at[y * 3 + g], yr.at[g, y], lsem.at[8 + g]))
    for c in yown:
        c.start()
    weights = [
        pltpu.make_async_copy(
            aops.at[k, pl.ds(pl.multiple_of(lo * 512, 512), 512), pl.ds(pl.multiple_of(half * 512 + b * A, A), A)],
            wa.at[j, b, pl.ds(k * 512, 512)], wsem.at[8 * k + 4 * j + b])
        for k in range(2) for j, half in enumerate((lo, 1 - lo)) for b in range(4)
    ]
    for w in weights:
        w.start()

    ks[...] = spread(sops[...].reshape(64, 32), 8)
    c_high, c_low = split_two(coup[...])
    ky[:, 0:192] = spread(c_high[0], 16)
    ky[:, 192:384] = spread(c_low[0], 16)
    kz[:, 0:192] = spread(c_high[1], 16)
    kz[:, 192:384] = spread(c_high[2], 16)
    kz[:, 384:576] = spread(c_low[1], 16)
    kz[:, 576:768] = spread(c_low[2], 16)
    h_high, h_low = split_two(chem[...])
    for c in range(3):
        high = spread(h_high[c], 16)
        kc[192 * c:192 * c + 192, 0:192] = high
        kc[192 * c:192 * c + 192, 192:384] = high
        kc[192 * c:192 * c + 192, 384:576] = spread(h_low[c], 16)
    for k in range(2):
        kn[96 * k:96 * k + 96] = nops[k, pl.ds(pl.multiple_of(ni * 96, 96), 96), :]

    def scale_of(first_row, rows):
        row = lax.broadcasted_iota(jnp.int32, (rows, A), 0) + first_row + ni * N
        return jnp.where(row == 0, 0.0, 0.2).astype(F32)

    def source(st):
        def pair(q, _):
            r0 = pl.multiple_of(q * 32, 32)
            p = jnp.concatenate([pert[:, st, pl.ds(r0, 16), :].reshape(192, A),
                                 pert[:, st, pl.ds(pl.multiple_of(r0 + 16, 16), 16), :].reshape(192, A)], axis=1)
            high = p.astype(BF16)
            low = (p - high.astype(F32)).astype(BF16)
            parts = jnp.dot(kc[...], jnp.concatenate([high, low, high], axis=0), preferred_element_type=F32)
            parts = parts.reshape(3, NV, 16, 2 * A)
            p = p.reshape(NV, 16, 2 * A)
            for j in range(2):
                rj = pl.multiple_of(r0 + 16 * j, 16)
                lanes = slice(j * A, (j + 1) * A)
                b5, b6, b7 = (base[f, st, pl.ds(rj, 16), :].astype(F32) for f in (5, 6, 7))
                held = scale_of(rj, 16)
                for v in range(NV):
                    here = p[v, :, lanes]
                    src = parts[0, v, :, lanes] + b5 * parts[1, v, :, lanes] + b6 * parts[2, v, :, lanes] - b7 * here
                    out[v, st, pl.ds(rj, 16), :] = here + (held if 5 <= v <= 9 else 0.2) * src
            return 0
        lax.fori_loop(0, 3, pair, 0, unroll=3)

    def sources(first, count):
        def one(i, _):
            source(i)
            return 0
        lax.fori_loop(first, first + count, one, 0)

    def stream_flux(g):
        for d in (1, 3, 2):
            yf(g, d).wait_recv()
        yown[g].wait()

        def derive(q, _):
            x = jnp.concatenate([yr[g, :, 2 * q].reshape(256, A), yr[g, :, 2 * q + 1].reshape(256, A)], axis=1)
            both = jnp.dot(ks[...], x, preferred_element_type=F32)
            for j in range(2):
                dy[0, 2 * q + j] = both[0:256, j * A:(j + 1) * A]
                dy[1, 2 * q + j] = both[256:512, j * A:(j + 1) * A]
            return 0

        lax.fori_loop(0, NV // 2, derive, 0, unroll=6)

        def mix(q, _):
            dst, pr = q // 2, q % 2
            row = lambda j: pl.multiple_of(dst * 64 + pr * 32 + 16 * j, 16)
            first = jnp.concatenate([dy[0, :, pl.ds(row(j), 16), :].reshape(192, A) for j in range(2)], axis=1)
            low = first.astype(BF16)
            mixed = jnp.dot(ky[...], jnp.concatenate([low, low], axis=0), preferred_element_type=F32)
            mixed = mixed.reshape(NV, 16, 2 * A)
            for j in range(2):
                lanes = slice(j * A, (j + 1) * A)
                near = pl.multiple_of(pr * 32 + 16 * j, 16)
                u, rho, nu = (yr[g, dst, NV + f, pl.ds(near, 16), :].astype(F32) for f in range(3))
                for v in range(NV):
                    d1, d2 = dy[0, v, pl.ds(row(j), 16), :], dy[1, v, pl.ds(row(j), 16), :]
                    flux = nu * d2 - u * d1 - rho * mixed[v, :, lanes]
                    fy[g, dst, v, pl.ds(near, 16), :] = flux.astype(BF16)
            return 0

        lax.fori_loop(0, 8, mix, 0, unroll=2)
        for d in (1, 3, 2):
            yret(g, d).start()

    def azimuth(t, own_blocks, other_blocks, fresh):
        def rows_of(q, _):
            r = pl.ds(pl.multiple_of(q * 16, 16), 16)
            x = [gat[t, slot_own, b, :, r, :].reshape(192, A) for b in own_blocks]
            x += [oth[t, b, :, r, :].reshape(192, A) for b in other_blocks]
            w = [wa[0, b] for b in own_blocks] + [wa[1, b] for b in other_blocks]
            both = lax.dot_general(jnp.concatenate(x, axis=1), jnp.concatenate(w, axis=1), (((1,), (1,)), ((), ())),
                                   preferred_element_type=F32)
            for k in range(2):
                for b in range(4):
                    part = both[:, k * 512 + b * A:k * 512 + (b + 1) * A].reshape(NV, 16, A)
                    if not fresh:
                        part = part + da[t, k, b, :, r, :]
                    da[t, k, b, :, r, :] = part
            return 0

        lax.fori_loop(0, N // 16, rows_of, 0, unroll=2)

    def turned_flux(t, d):
        b = z_of(-d)
        co(t, d).wait_recv()
        cw(t, d).wait_recv()
        if d:
            zb(t, d).wait_recv()

        def normal(q, _):
            x = jnp.concatenate([gat[t, :, b, 2 * q].reshape(384, A), gat[t, :, b, 2 * q + 1].reshape(384, A)], axis=1)
            both = jnp.dot(kn[...], x, preferred_element_type=F32)
            for j in range(2):
                for k in range(2):
                    dn[k, 2 * q + j] = both[96 * k:96 * k + 96, j * A:(j + 1) * A]
            return 0

        lax.fori_loop(0, NV // 2, normal, 0, unroll=6)

        def mix(q, _):
            rs = [pl.ds(pl.multiple_of(q * 32 + 16 * j, 16), 16) for j in range(2)]
            low_a = jnp.concatenate([da[t, 0, b, :, r, :].reshape(192, A) for r in rs], axis=1).astype(BF16)
            low_n = jnp.concatenate([dn[0, :, r, :].reshape(192, A) for r in rs], axis=1).astype(BF16)
            mixed = jnp.dot(kz[...], jnp.concatenate([low_a, low_n, low_a, low_n], axis=0), preferred_element_type=F32)
            for j, r in enumerate(rs):
                lanes = slice(j * A, (j + 1) * A)
                u1, u2, rho, nu = (zbase[t, b, f, r, :].astype(F32) for f in range(4))
                for v in range(NV):
                    flux = (nu * (da[t, 1, b, v, r, :] + dn[1, v, r, :]) - u1 * da[t, 0, b, v, r, :] - u2 * dn[0, v, r, :]
                            - rho * mixed[16 * v:16 * v + 16, lanes])
                    fz[t, b, v, r, :] = flux.astype(BF16)
            return 0

        lax.fori_loop(0, N // 32, mix, 0, unroll=3)
        if d:
            zr(t, 4 - d).start()

    def pass_lo(t, d):
        zf(t, d).wait_recv()
        lo_c(t, d).start()
        co(t, d).start()

    def pass_hi(t, d):
        lo_c(t, d).wait_recv()
        hi_c(t, d).start()

    def pass_core(t, d):
        hi_c(t, d).wait_recv()
        cw(t, d).start()

    def add_stream(g, d):
        i = y_of(-d) * 3 + g
        r = pl.ds(pl.multiple_of(i * 8, 8), 8)
        held = scale_of(i * 8, 8)
        for v in range(NV):
            src = fy[g, y, v] if d == 0 else ry[i, v]
            out[v, :, r, :] += (held if 5 <= v <= 9 else 0.2) * src.astype(F32).reshape(S, 8, A)

    def add_turned(t, d):
        st = 2 * z_of(-d) + t
        held = scale_of(0, N)
        for v in range(NV):
            src = fz[t, z, v] if d == 0 else rz[st, v]
            out[v, st] += (held if 5 <= v <= 9 else 0.2) * src.astype(F32)

    order = [(0, 0), (1, 0), (0, 1), (0, 3), (0, 2), (1, 1), (1, 3), (1, 2)]

    def step(k):
        pass_hi(*order[k])
        if k + 2 < 8:
            pass_lo(*order[k + 2])
        if 2 <= k < 7:
            pass_core(*order[k - 2])

    sources(0, 3)
    step(0)
    sources(3, 3)
    step(1)
    sources(6, 2)
    step(2)
    stream_flux(0)
    step(3)
    stream_flux(1)
    for w in weights:
        w.wait()
    for c in own:
        c.wait()
    step(4)
    azimuth(0, range(4), range(4), True)
    stream_flux(2)
    step(5)
    turned_flux(0, 0)
    turned_flux(0, 1)
    azimuth(1, range(4), [z_of(-d) for d in (0, 1)], True)
    step(6)
    turned_flux(0, 3)
    turned_flux(0, 2)
    pass_core(1, 1)
    step(7)
    azimuth(1, [], [z_of(-d) for d in (3, 2)], False)
    turned_flux(1, 1)
    pass_core(1, 3)
    turned_flux(1, 3)
    turned_flux(1, 0)
    pass_core(1, 2)
    turned_flux(1, 2)
    for g in range(3):
        add_stream(g, 0)
        for d in (1, 3, 2):
            yret(g, d).wait_recv()
            add_stream(g, d)
    for t in range(2):
        for d in (0, 1, 3, 2):
            if d:
                zr(t, d).wait_recv()
            add_turned(t, d)
    for t in range(2):
        for d in range(4):
            for copy in (lo_c, co, hi_c, cw):
                copy(t, d).wait_send()
        for d in (1, 2, 3):
            for copy in (zf, zb, zr):
                copy(t, d).wait_send()
    for g in range(3):
        for d in (1, 2, 3):
            yf(g, d).wait_send()
            yret(g, d).wait_send()


def shards(perturbation, base_flow, stream_ops, azimuth_ops, normal_ops, coupling, chemistry):
    vmem = pl.BlockSpec(memory_space=pltpu.VMEM)
    hbm = pl.BlockSpec(memory_space=pl.ANY)
    scratch = lambda *shape: pltpu.VMEM(shape, BF16)
    return pl.pallas_call(
        kernel,
        out_shape=pltpu.VMEM(perturbation.shape, F32),
        in_specs=[hbm, hbm, vmem, hbm, vmem, vmem, vmem],
        out_specs=vmem,
        scratch_shapes=[
            pltpu.VMEM((NV, S, N, A), F32),
            scratch(8, S, N, A),
            scratch(S, NV, N, A),
            scratch(S, 4, N, A),
            scratch(2, 4, 4, NV, N, A),
            scratch(2, 4, 4, N, A),
            scratch(2, 4, NV, N, A),
            scratch(12, 15, 64, A),
            scratch(3, 4, 15, 64, A),
            scratch(3, 4, NV, 64, A),
            scratch(12, NV, 64, A),
            scratch(2, 4, NV, N, A),
            scratch(S, NV, N, A),
            pltpu.VMEM((2, 2, 4, NV, N, A), F32),
            pltpu.VMEM((2, NV, N, A), F32),
            pltpu.VMEM((2, NV, 256, A), F32),
            scratch(2, 4, 1024, A),
            scratch(576, 576),
            scratch(192, 384),
            scratch(192, 768),
            scratch(512, 256),
            scratch(192, 384),
            pltpu.SemaphoreType.DMA((COPIES,)),
            pltpu.SemaphoreType.DMA((COPIES,)),
            pltpu.SemaphoreType.DMA((11,)),
            pltpu.SemaphoreType.DMA((2 * S,)),
            pltpu.SemaphoreType.DMA((16,)),
        ],
        compiler_params=pltpu.CompilerParams(collective_id=0, has_side_effects=True, vmem_limit_bytes=56 << 20),
    )(perturbation, base_flow, stream_ops, azimuth_ops, normal_ops, coupling, chemistry)


def solution(mesh):
    field = P(None, "stream", "normal", "azim")
    return jax.shard_map(
        shards,
        mesh=mesh,
        in_specs=(field, field, P(), P(), P(), P(), P()),
        out_specs=field,
        check_vma=False,
    )
```

```python
import functools

import jax
import jax.numpy as jnp
from jax import lax
from jax.experimental import pallas as pl
from jax.experimental.pallas import tpu as pltpu
from jax.sharding import PartitionSpec as P

MESH = pl.DeviceIdType.MESH
F32, BF16 = jnp.float32, jnp.bfloat16
NV, S, N, A = 12, 8, 96, 128


def copies_table():
    table, count = {}, 0
    for t in range(2):
        for d in (1, 2, 3):
            for name in ("zf", "zb", "zr"):
                table[name, t, d] = count
                count += 1
        for d in range(4):
            for name in ("co", "cw"):
                table[name, t, d] = count
                count += 1
            for part in range(2):
                for name in ("lo", "hi"):
                    table[name, t, d, part] = count
                    count += 1
    for g in range(3):
        for d in (1, 2, 3):
            for name in ("yf", "yr"):
                table[name, g, d] = count
                count += 1
    return table, count


TABLE, COPIES = copies_table()


def spread(matrix, reps):
    rows, cols = matrix.shape
    shift = reps.bit_length() - 1
    up = (lax.broadcasted_iota(jnp.int32, (rows * reps, rows), 0) >> shift
          == lax.broadcasted_iota(jnp.int32, (rows * reps, rows), 1)).astype(F32).astype(BF16)
    wide = (lax.broadcasted_iota(jnp.int32, (cols, cols * reps), 1) >> shift
            == lax.broadcasted_iota(jnp.int32, (cols, cols * reps), 0)).astype(F32).astype(BF16)
    tall = jnp.dot(up, matrix, preferred_element_type=F32).astype(BF16)
    full = jnp.dot(tall, wide, preferred_element_type=F32)
    r = lax.broadcasted_iota(jnp.int32, full.shape, 0) & (reps - 1)
    c = lax.broadcasted_iota(jnp.int32, full.shape, 1) & (reps - 1)
    return jnp.where(r == c, full, 0.0).astype(BF16)


def split_two(matrix):
    high = matrix.astype(BF16)
    return high, (matrix - high.astype(F32)).astype(BF16)


def kernel(pert_hbm, base_hbm, sops, aops, nops, coup, chem, out,
           pert, base, zs, zbs, gat, zbase, oth, ys, yr, fy, ry, fz, rz, da, dn, dy, wa, kc, ky, kz, ks, kn,
           ssem, rsem, lsem, isem, wsem):
    y = lax.axis_index("stream")
    ai = lax.axis_index("azim")
    ni = lax.axis_index("normal")
    lo, z = ai // 4, ai % 4
    hi, core = ni // 2, ni % 2

    def at(y_=None, z_=None, lo_=None, hi_=None, core_=None):
        pick = lambda new, old: old if new is None else new
        return {"stream": pick(y_, y), "azim": pick(lo_, lo) * 4 + pick(z_, z),
                "normal": pick(hi_, hi) * 2 + pick(core_, core)}

    y_of = lambda d: (y + d) % 4
    z_of = lambda d: (z + d) % 4
    lo_dev = at(lo_=1 - lo)
    hi_dev = at(lo_=1 - lo, hi_=1 - hi)
    core_dev = at(core_=1 - core)
    slot_own = ni
    slot_core = hi * 2 + (1 - core)
    slot_hi = (1 - hi) * 2 + core
    slot_both = (1 - hi) * 2 + (1 - core)

    stations = [2 * z_of(d) + t for t in range(2) for d in (0, 1, 3, 2)]
    loads = [(pltpu.make_async_copy(pert_hbm.at[:, st], pert.at[:, st], isem.at[2 * i]),
              pltpu.make_async_copy(base_hbm.at[:, st], base.at[:, st], isem.at[2 * i + 1]))
             for i, st in enumerate(stations)]
    for pair in loads:
        for load in pair:
            load.start()
    barrier = pltpu.get_barrier_semaphore()
    partners = [at(y_=y_of(d)) for d in (1, 2, 3)] + [at(z_=z_of(d)) for d in (1, 2, 3)] + [lo_dev, hi_dev, core_dev]
    for device in partners:
        pl.semaphore_signal(barrier, inc=1, device_id=device, device_id_type=MESH)

    def remote(src, dst, key, device):
        i = TABLE[key]
        return pltpu.make_async_remote_copy(src_ref=src, dst_ref=dst, send_sem=ssem.at[i], recv_sem=rsem.at[i],
                                            device_id=device, device_id_type=MESH)

    def zf(t, d):
        return remote(zs.at[2 * z_of(d) + t], gat.at[t, slot_own, z], ("zf", t, d), at(z_=z_of(d)))

    def zb(t, d):
        return remote(zbs.at[2 * z_of(d) + t], zbase.at[t, z], ("zb", t, d), at(z_=z_of(d)))

    def zr(t, d):
        return remote(fz.at[t, z_of(d)], rz.at[2 * z + t], ("zr", t, d), at(z_=z_of(d)))

    def src_own(t, d):
        return zs.at[2 * z + t] if d == 0 else gat.at[t, slot_own, z_of(-d)]

    def piece(ref, part):
        return ref.at[pl.ds(part * (NV // 2), NV // 2)]

    def lo_c(t, d, part):
        return remote(piece(src_own(t, d), part), piece(oth.at[t, z_of(-d)], part), ("lo", t, d, part), lo_dev)

    def co(t, d):
        return remote(src_own(t, d), gat.at[t, slot_own, z_of(-d)], ("co", t, d), core_dev)

    def hi_c(t, d, part):
        return remote(piece(oth.at[t, z_of(-d)], part), piece(gat.at[t, slot_own, z_of(-d)], part), ("hi", t, d, part), hi_dev)

    def cw(t, d):
        return remote(gat.at[t, slot_hi, z_of(-d)], gat.at[t, slot_hi, z_of(-d)], ("cw", t, d), core_dev)

    def yf(g, d):
        return remote(ys.at[y_of(d) * 3 + g], yr.at[g, y], ("yf", g, d), at(y_=y_of(d)))

    def yret(g, d):
        return remote(fy.at[g, y_of(d)], ry.at[y * 3 + g], ("yr", g, d), at(y_=y_of(d)))

    def lower(i):
        for load in loads[i]:
            load.wait()
        st = stations[i]
        zs[st] = pert[:, st].astype(BF16)
        for f in range(4):
            zbs[st, f] = base[1 + f, st]

    lower(0)
    pl.semaphore_wait(barrier, len(partners))
    for part in range(2):
        lo_c(0, 0, part).start()
    co(0, 0).start()
    for i, d in enumerate((1, 3, 2)):
        lower(1 + i)
        zf(0, d).start()
    lower(4)
    co(1, 0).start()
    for i in (5, 6, 7):
        lower(i)
    own = []
    for t in range(2):
        own.append(pltpu.make_async_copy(zs.at[2 * z + t], gat.at[t, slot_own, z], lsem.at[4 + t]))
        own.append(pltpu.make_async_copy(zbs.at[2 * z + t], zbase.at[t, z], lsem.at[6 + t]))
    for c in own:
        c.start()

    def lower_y(i, _):
        rows = pert[:, :, pl.ds(pl.multiple_of(i * 8, 8), 8), :]
        ys[i, 0:NV] = rows.reshape(NV, 64, A).astype(BF16)
        return 0

    lax.fori_loop(0, 12, lower_y, 0)
    for j, f in enumerate((0, 3, 4)):
        wide = base[f].astype(F32)
        for i in range(12):
            ys[i, NV + j] = wide[:, 8 * i:8 * i + 8, :].reshape(64, A).astype(BF16)
    for g in range(3):
        for d in (1, 3, 2):
            yf(g, d).start()
    for d in (1, 3, 2):
        zf(1, d).start()
    for t in range(2):
        for d in (1, 3, 2):
            zb(t, d).start()
    yown = []
    for g in range(3):
        yown.append(pltpu.make_async_copy(ys.at[y * 3 + g], yr.at[g, y], lsem.at[8 + g]))
    for c in yown:
        c.start()
    weights = [
        pltpu.make_async_copy(
            aops.at[k, pl.ds(pl.multiple_of(lo * 512, 512), 512), pl.ds(pl.multiple_of(half * 512 + b * A, A), A)],
            wa.at[j, b, pl.ds(k * 512, 512)], wsem.at[8 * k + 4 * j + b])
        for k in range(2) for j, half in enumerate((lo, 1 - lo)) for b in range(4)
    ]
    for w in weights:
        w.start()

    ks[...] = spread(sops[...].reshape(64, 32), 8)
    c_high, c_low = split_two(coup[...])
    ky[:, 0:192] = spread(c_high[0], 16)
    ky[:, 192:384] = spread(c_low[0], 16)
    kz[:, 0:192] = spread(c_high[1], 16)
    kz[:, 192:384] = spread(c_high[2], 16)
    kz[:, 384:576] = spread(c_low[1], 16)
    kz[:, 576:768] = spread(c_low[2], 16)
    h_high, h_low = split_two(chem[...])
    for c in range(3):
        high = spread(h_high[c], 16)
        kc[192 * c:192 * c + 192, 0:192] = high
        kc[192 * c:192 * c + 192, 192:384] = high
        kc[192 * c:192 * c + 192, 384:576] = spread(h_low[c], 16)
    for k in range(2):
        kn[96 * k:96 * k + 96] = nops[k, pl.ds(pl.multiple_of(ni * 96, 96), 96), :]

    def scale_of(first_row, rows):
        row = lax.broadcasted_iota(jnp.int32, (rows, A), 0) + first_row + ni * N
        return jnp.where(row == 0, 0.0, 0.2).astype(F32)

    def source(st):
        def pair(q, _):
            r0 = pl.multiple_of(q * 32, 32)
            p = jnp.concatenate([pert[:, st, pl.ds(r0, 16), :].reshape(192, A),
                                 pert[:, st, pl.ds(pl.multiple_of(r0 + 16, 16), 16), :].reshape(192, A)], axis=1)
            high = p.astype(BF16)
            low = (p - high.astype(F32)).astype(BF16)
            parts = jnp.dot(kc[...], jnp.concatenate([high, low, high], axis=0), preferred_element_type=F32)
            parts = parts.reshape(3, NV, 16, 2 * A)
            p = p.reshape(NV, 16, 2 * A)
            for j in range(2):
                rj = pl.multiple_of(r0 + 16 * j, 16)
                lanes = slice(j * A, (j + 1) * A)
                b5, b6, b7 = (base[f, st, pl.ds(rj, 16), :].astype(F32) for f in (5, 6, 7))
                held = scale_of(rj, 16)
                for v in range(NV):
                    here = p[v, :, lanes]
                    src = parts[0, v, :, lanes] + b5 * parts[1, v, :, lanes] + b6 * parts[2, v, :, lanes] - b7 * here
                    out[v, st, pl.ds(rj, 16), :] = here + (held if 5 <= v <= 9 else 0.2) * src
            return 0
        lax.fori_loop(0, 3, pair, 0, unroll=3)

    def sources(first, count):
        def one(i, _):
            source(i)
            return 0
        lax.fori_loop(first, first + count, one, 0)

    def stream_flux(g):
        for d in (1, 3, 2):
            yf(g, d).wait_recv()
        yown[g].wait()

        def derive(q, _):
            x = jnp.concatenate([yr[g, :, 2 * q].reshape(256, A), yr[g, :, 2 * q + 1].reshape(256, A)], axis=1)
            both = jnp.dot(ks[...], x, preferred_element_type=F32)
            for j in range(2):
                dy[0, 2 * q + j] = both[0:256, j * A:(j + 1) * A]
                dy[1, 2 * q + j] = both[256:512, j * A:(j + 1) * A]
            return 0

        lax.fori_loop(0, NV // 2, derive, 0, unroll=6)

        def mix(q, _):
            dst, pr = q // 2, q % 2
            row = lambda j: pl.multiple_of(dst * 64 + pr * 32 + 16 * j, 16)
            first = jnp.concatenate([dy[0, :, pl.ds(row(j), 16), :].reshape(192, A) for j in range(2)], axis=1)
            low = first.astype(BF16)
            mixed = jnp.dot(ky[...], jnp.concatenate([low, low], axis=0), preferred_element_type=F32)
            mixed = mixed.reshape(NV, 16, 2 * A)
            for j in range(2):
                lanes = slice(j * A, (j + 1) * A)
                near = pl.multiple_of(pr * 32 + 16 * j, 16)
                u, rho, nu = (yr[g, dst, NV + f, pl.ds(near, 16), :].astype(F32) for f in range(3))
                for v in range(NV):
                    d1, d2 = dy[0, v, pl.ds(row(j), 16), :], dy[1, v, pl.ds(row(j), 16), :]
                    flux = nu * d2 - u * d1 - rho * mixed[v, :, lanes]
                    fy[g, dst, v, pl.ds(near, 16), :] = flux.astype(BF16)
            return 0

        lax.fori_loop(0, 8, mix, 0, unroll=2)
        for d in (1, 3, 2):
            yret(g, d).start()

    def azimuth(t, own_blocks, other_blocks, fresh, rows=(0, N // 16)):
        def rows_of(q, _):
            r = pl.ds(pl.multiple_of(q * 16, 16), 16)
            x = [gat[t, slot_own, b, :, r, :].reshape(192, A) for b in own_blocks]
            x += [oth[t, b, :, r, :].reshape(192, A) for b in other_blocks]
            w = [wa[0, b] for b in own_blocks] + [wa[1, b] for b in other_blocks]
            both = lax.dot_general(jnp.concatenate(x, axis=1), jnp.concatenate(w, axis=1), (((1,), (1,)), ((), ())),
                                   preferred_element_type=F32)
            for k in range(2):
                for b in range(4):
                    part = both[:, k * 512 + b * A:k * 512 + (b + 1) * A].reshape(NV, 16, A)
                    if not fresh:
                        part = part + da[t, k, b, :, r, :]
                    da[t, k, b, :, r, :] = part
            return 0

        lax.fori_loop(*rows, rows_of, 0, unroll=3)

    def turned_flux(t, d):
        b = z_of(-d)
        co(t, d).wait_recv()
        cw(t, d).wait_recv()
        if d:
            zb(t, d).wait_recv()

        def normal(q, _):
            x = jnp.concatenate([gat[t, :, b, 2 * q].reshape(384, A), gat[t, :, b, 2 * q + 1].reshape(384, A)], axis=1)
            both = jnp.dot(kn[...], x, preferred_element_type=F32)
            for j in range(2):
                for k in range(2):
                    dn[k, 2 * q + j] = both[96 * k:96 * k + 96, j * A:(j + 1) * A]
            return 0

        lax.fori_loop(0, NV // 2, normal, 0, unroll=6)

        def mix(q, _):
            rs = [pl.ds(pl.multiple_of(q * 32 + 16 * j, 16), 16) for j in range(2)]
            low_a = jnp.concatenate([da[t, 0, b, :, r, :].reshape(192, A) for r in rs], axis=1).astype(BF16)
            low_n = jnp.concatenate([dn[0, :, r, :].reshape(192, A) for r in rs], axis=1).astype(BF16)
            mixed = jnp.dot(kz[...], jnp.concatenate([low_a, low_n, low_a, low_n], axis=0), preferred_element_type=F32)
            for j, r in enumerate(rs):
                lanes = slice(j * A, (j + 1) * A)
                u1, u2, rho, nu = (zbase[t, b, f, r, :].astype(F32) for f in range(4))
                for v in range(NV):
                    flux = (nu * (da[t, 1, b, v, r, :] + dn[1, v, r, :]) - u1 * da[t, 0, b, v, r, :] - u2 * dn[0, v, r, :]
                            - rho * mixed[16 * v:16 * v + 16, lanes])
                    fz[t, b, v, r, :] = flux.astype(BF16)
            return 0

        lax.fori_loop(0, N // 32, mix, 0, unroll=3)
        if d:
            zr(t, 4 - d).start()

    def pass_lo(t, d, part):
        if d and not part:
            zf(t, d).wait_recv()
            co(t, d).start()
        lo_c(t, d, part).start()

    def pass_hi(t, d, part):
        lo_c(t, d, part).wait_recv()
        hi_c(t, d, part).start()

    def pass_core(t, d):
        for part in range(2):
            hi_c(t, d, part).wait_recv()
        cw(t, d).start()

    def add_stream(g, d):
        i = y_of(-d) * 3 + g
        r = pl.ds(pl.multiple_of(i * 8, 8), 8)
        held = scale_of(i * 8, 8)
        for v in range(NV):
            src = fy[g, y, v] if d == 0 else ry[i, v]
            out[v, :, r, :] += (held if 5 <= v <= 9 else 0.2) * src.astype(F32).reshape(S, 8, A)

    def add_turned(t, d):
        st = 2 * z_of(-d) + t
        held = scale_of(0, N)
        for v in range(NV):
            src = fz[t, z, v] if d == 0 else rz[st, v]
            out[v, st] += (held if 5 <= v <= 9 else 0.2) * src.astype(F32)

    order = [(0, 0, 0), (0, 0, 1), (1, 0, 0)]
    order += [(t, d, part) for t in range(2) for d in ((1, 3, 2)) for part in range(2)] + [(1, 0, 1)]

    def step(k):
        pass_hi(*order[k])
        if k + 2 < len(order):
            pass_lo(*order[k + 2])

    first, second = (0, N // 32), (N // 32, N // 16)
    sources(0, 2)
    step(0)
    sources(2, 1)
    step(1)
    sources(3, 1)
    step(2)
    sources(4, 1)
    step(3)
    sources(5, 1)
    step(4)
    pass_core(0, 0)
    sources(6, 2)
    step(5)
    step(6)
    stream_flux(0)
    step(7)
    pass_core(0, 1)
    stream_flux(1)
    for w in weights:
        w.wait()
    for c in own:
        c.wait()
    step(8)
    azimuth(0, range(4), range(4), True, first)
    pass_core(0, 3)
    step(9)
    azimuth(0, range(4), range(4), True, second)
    step(10)
    turned_flux(0, 0)
    turned_flux(0, 1)
    pass_core(0, 2)
    step(11)
    turned_flux(0, 3)
    stream_flux(2)
    step(12)
    turned_flux(0, 2)
    pass_core(1, 1)
    azimuth(1, range(4), [z_of(-d) for d in (1, 3)], True, first)
    step(13)
    azimuth(1, range(4), [z_of(-d) for d in (1, 3)], True, second)
    step(14)
    pass_core(1, 3)
    step(15)
    azimuth(1, [], [z_of(-d) for d in (2, 0)], False)
    turned_flux(1, 1)
    turned_flux(1, 3)
    pass_core(1, 2)
    turned_flux(1, 2)
    pass_core(1, 0)
    turned_flux(1, 0)
    for g in range(3):
        add_stream(g, 0)
        for d in (1, 3, 2):
            yret(g, d).wait_recv()
            add_stream(g, d)
    for t in range(2):
        for d in (0, 1, 3, 2):
            if d:
                zr(t, d).wait_recv()
            add_turned(t, d)
    for t in range(2):
        for d in range(4):
            for copy in (co, cw):
                copy(t, d).wait_send()
            for part in range(2):
                lo_c(t, d, part).wait_send()
                hi_c(t, d, part).wait_send()
        for d in (1, 2, 3):
            for copy in (zf, zb, zr):
                copy(t, d).wait_send()
    for g in range(3):
        for d in (1, 2, 3):
            yf(g, d).wait_send()
            yret(g, d).wait_send()


def shards(perturbation, base_flow, stream_ops, azimuth_ops, normal_ops, coupling, chemistry):
    vmem = pl.BlockSpec(memory_space=pltpu.VMEM)
    hbm = pl.BlockSpec(memory_space=pl.ANY)
    scratch = lambda *shape: pltpu.VMEM(shape, BF16)
    return pl.pallas_call(
        kernel,
        out_shape=pltpu.VMEM(perturbation.shape, F32),
        in_specs=[hbm, hbm, vmem, hbm, vmem, vmem, vmem],
        out_specs=vmem,
        scratch_shapes=[
            pltpu.VMEM((NV, S, N, A), F32),
            scratch(8, S, N, A),
            scratch(S, NV, N, A),
            scratch(S, 4, N, A),
            scratch(2, 4, 4, NV, N, A),
            scratch(2, 4, 4, N, A),
            scratch(2, 4, NV, N, A),
            scratch(12, 15, 64, A),
            scratch(3, 4, 15, 64, A),
            scratch(3, 4, NV, 64, A),
            scratch(12, NV, 64, A),
            scratch(2, 4, NV, N, A),
            scratch(S, NV, N, A),
            pltpu.VMEM((2, 2, 4, NV, N, A), F32),
            pltpu.VMEM((2, NV, N, A), F32),
            pltpu.VMEM((2, NV, 256, A), F32),
            scratch(2, 4, 1024, A),
            scratch(576, 576),
            scratch(192, 384),
            scratch(192, 768),
            scratch(512, 256),
            scratch(192, 384),
            pltpu.SemaphoreType.DMA((COPIES,)),
            pltpu.SemaphoreType.DMA((COPIES,)),
            pltpu.SemaphoreType.DMA((11,)),
            pltpu.SemaphoreType.DMA((2 * S,)),
            pltpu.SemaphoreType.DMA((16,)),
        ],
        compiler_params=pltpu.CompilerParams(collective_id=0, has_side_effects=True, vmem_limit_bytes=56 << 20),
    )(perturbation, base_flow, stream_ops, azimuth_ops, normal_ops, coupling, chemistry)


def solution(mesh):
    field = P(None, "stream", "normal", "azim")
    return jax.shard_map(
        shards,
        mesh=mesh,
        in_specs=(field, field, P(), P(), P(), P(), P()),
        out_specs=field,
        check_vma=False,
    )
```

```python
import functools

import jax
import jax.numpy as jnp
from jax import lax
from jax.experimental import pallas as pl
from jax.experimental.pallas import tpu as pltpu
from jax.sharding import PartitionSpec as P

MESH = pl.DeviceIdType.MESH
F32, BF16 = jnp.float32, jnp.bfloat16
NV, S, N, A = 12, 8, 96, 128


PARTS = 4


def copies_table():
    table, count = {}, 0
    for t in range(2):
        for d in (1, 2, 3):
            for name in ("zf", "zb", "zr"):
                table[name, t, d] = count
                count += 1
        for d in range(4):
            table["co", t, d] = count
            count += 1
            for part in range(2):
                table["cw", t, d, part] = count
                count += 1
            for part in range(PARTS):
                for name in ("lo", "hi"):
                    table[name, t, d, part] = count
                    count += 1
    for g in range(3):
        for d in (1, 2, 3):
            for name in ("yf", "yr"):
                table[name, g, d] = count
                count += 1
    return table, count


TABLE, COPIES = copies_table()


def spread(matrix, reps):
    rows, cols = matrix.shape
    shift = reps.bit_length() - 1
    up = (lax.broadcasted_iota(jnp.int32, (rows * reps, rows), 0) >> shift
          == lax.broadcasted_iota(jnp.int32, (rows * reps, rows), 1)).astype(F32).astype(BF16)
    wide = (lax.broadcasted_iota(jnp.int32, (cols, cols * reps), 1) >> shift
            == lax.broadcasted_iota(jnp.int32, (cols, cols * reps), 0)).astype(F32).astype(BF16)
    tall = jnp.dot(up, matrix, preferred_element_type=F32).astype(BF16)
    full = jnp.dot(tall, wide, preferred_element_type=F32)
    r = lax.broadcasted_iota(jnp.int32, full.shape, 0) & (reps - 1)
    c = lax.broadcasted_iota(jnp.int32, full.shape, 1) & (reps - 1)
    return jnp.where(r == c, full, 0.0).astype(BF16)


def split_two(matrix):
    high = matrix.astype(BF16)
    return high, (matrix - high.astype(F32)).astype(BF16)


def kernel(pert_hbm, base_hbm, sops_hbm, aops, nops_hbm, coup_hbm, chem_hbm, out,
           pert, base, sops, nops, coup, chem, zs, zbs, gat, zbase, oth, ys, yr, fy, ry, fz, rz, da, dn, dy, wa, kc, ky, kz, ks, kn,
           ssem, rsem, lsem, isem, wsem):
    y = lax.axis_index("stream")
    ai = lax.axis_index("azim")
    ni = lax.axis_index("normal")
    lo, z = ai // 4, ai % 4
    hi, core = ni // 2, ni % 2

    def at(y_=None, z_=None, lo_=None, hi_=None, core_=None):
        pick = lambda new, old: old if new is None else new
        return {"stream": pick(y_, y), "azim": pick(lo_, lo) * 4 + pick(z_, z),
                "normal": pick(hi_, hi) * 2 + pick(core_, core)}

    y_of = lambda d: (y + d) % 4
    z_of = lambda d: (z + d) % 4
    lo_dev = at(lo_=1 - lo)
    hi_dev = at(lo_=1 - lo, hi_=1 - hi)
    core_dev = at(core_=1 - core)
    slot_own = ni
    slot_core = hi * 2 + (1 - core)
    slot_hi = (1 - hi) * 2 + core
    slot_both = (1 - hi) * 2 + (1 - core)

    stations = [2 * z_of(d) + t for t in range(2) for d in (0, 1, 3, 2)]
    loads = [(pltpu.make_async_copy(pert_hbm.at[:, st], pert.at[:, st], isem.at[2 * i]),
              pltpu.make_async_copy(base_hbm.at[:, st], base.at[:, st], isem.at[2 * i + 1]))
             for i, st in enumerate(stations)]
    for pair in loads:
        for load in pair:
            load.start()
    small = [pltpu.make_async_copy(far, near, isem.at[2 * S + i]) for i, (far, near) in enumerate(
        ((sops_hbm, sops), (nops_hbm, nops), (coup_hbm, coup), (chem_hbm, chem)))]
    for load in small:
        load.start()
    barrier = pltpu.get_barrier_semaphore()
    partners = [at(y_=y_of(d)) for d in (1, 2, 3)] + [at(z_=z_of(d)) for d in (1, 2, 3)] + [lo_dev, hi_dev, core_dev]
    for device in partners:
        pl.semaphore_signal(barrier, inc=1, device_id=device, device_id_type=MESH)

    def remote(src, dst, key, device):
        i = TABLE[key]
        return pltpu.make_async_remote_copy(src_ref=src, dst_ref=dst, send_sem=ssem.at[i], recv_sem=rsem.at[i],
                                            device_id=device, device_id_type=MESH)

    def zf(t, d):
        return remote(zs.at[2 * z_of(d) + t], gat.at[t, slot_own, z], ("zf", t, d), at(z_=z_of(d)))

    def zb(t, d):
        return remote(zbs.at[2 * z_of(d) + t], zbase.at[t, z], ("zb", t, d), at(z_=z_of(d)))

    def zr(t, d):
        return remote(fz.at[t, z_of(d)], rz.at[2 * z + t], ("zr", t, d), at(z_=z_of(d)))

    def src_own(t, d):
        return zs.at[2 * z + t] if d == 0 else gat.at[t, slot_own, z_of(-d)]

    def piece(ref, part, parts=PARTS):
        return ref.at[pl.ds(part * (NV // parts), NV // parts)]

    def lo_c(t, d, part):
        return remote(piece(src_own(t, d), part), piece(oth.at[t, z_of(-d)], part), ("lo", t, d, part), lo_dev)

    def co(t, d):
        return remote(src_own(t, d), gat.at[t, slot_own, z_of(-d)], ("co", t, d), core_dev)

    def hi_c(t, d, part):
        return remote(piece(oth.at[t, z_of(-d)], part), piece(gat.at[t, slot_own, z_of(-d)], part), ("hi", t, d, part), hi_dev)

    def cw(t, d, part):
        here = piece(gat.at[t, slot_hi, z_of(-d)], part, 2)
        return remote(here, here, ("cw", t, d, part), core_dev)

    def yf(g, d):
        return remote(ys.at[y_of(d) * 3 + g], yr.at[g, y], ("yf", g, d), at(y_=y_of(d)))

    def yret(g, d):
        return remote(fy.at[g, y_of(d)], ry.at[y * 3 + g], ("yr", g, d), at(y_=y_of(d)))

    def lower(i):
        for load in loads[i]:
            load.wait()
        st = stations[i]
        zs[st] = pert[:, st].astype(BF16)
        for f in range(4):
            zbs[st, f] = base[1 + f, st]

    lower(0)
    pl.semaphore_wait(barrier, len(partners))
    for part in range(PARTS):
        lo_c(0, 0, part).start()
    co(0, 0).start()
    for i, d in enumerate((1, 3, 2)):
        lower(1 + i)
        zf(0, d).start()
    lower(4)
    co(1, 0).start()
    for i in (5, 6, 7):
        lower(i)
    own = []
    for t in range(2):
        own.append(pltpu.make_async_copy(zs.at[2 * z + t], gat.at[t, slot_own, z], lsem.at[4 + t]))
        own.append(pltpu.make_async_copy(zbs.at[2 * z + t], zbase.at[t, z], lsem.at[6 + t]))
    for c in own:
        c.start()

    def lower_y(i, _):
        rows = pert[:, :, pl.ds(pl.multiple_of(i * 8, 8), 8), :]
        ys[i, 0:NV] = rows.reshape(NV, 64, A).astype(BF16)
        return 0

    lax.fori_loop(0, 12, lower_y, 0)
    for j, f in enumerate((0, 3, 4)):
        wide = base[f].astype(F32)
        for i in range(12):
            ys[i, NV + j] = wide[:, 8 * i:8 * i + 8, :].reshape(64, A).astype(BF16)
    for g in range(3):
        for d in (1, 3, 2):
            yf(g, d).start()
    for d in (1, 3, 2):
        zf(1, d).start()
    for t in range(2):
        for d in (1, 3, 2):
            zb(t, d).start()
    yown = []
    for g in range(3):
        yown.append(pltpu.make_async_copy(ys.at[y * 3 + g], yr.at[g, y], lsem.at[8 + g]))
    for c in yown:
        c.start()
    weights = [
        pltpu.make_async_copy(
            aops.at[k, pl.ds(pl.multiple_of(lo * 512, 512), 512), pl.ds(pl.multiple_of(half * 512 + b * A, A), A)],
            wa.at[j, b, pl.ds(k * 512, 512)], wsem.at[8 * k + 4 * j + b])
        for k in range(2) for j, half in enumerate((lo, 1 - lo)) for b in range(4)
    ]
    for w in weights:
        w.start()

    for load in small:
        load.wait()
    ks[...] = spread(sops[...].reshape(64, 32), 8)
    c_high, c_low = split_two(coup[...])
    ky[:, 0:192] = spread(c_high[0], 16)
    ky[:, 192:384] = spread(c_low[0], 16)
    kz[:, 0:192] = spread(c_high[1], 16)
    kz[:, 192:384] = spread(c_high[2], 16)
    kz[:, 384:576] = spread(c_low[1], 16)
    kz[:, 576:768] = spread(c_low[2], 16)
    h_high, h_low = split_two(chem[...])
    for c in range(3):
        high = spread(h_high[c], 16)
        kc[192 * c:192 * c + 192, 0:192] = high
        kc[192 * c:192 * c + 192, 192:384] = high
        kc[192 * c:192 * c + 192, 384:576] = spread(h_low[c], 16)
    for k in range(2):
        kn[96 * k:96 * k + 96] = nops[k, pl.ds(pl.multiple_of(ni * 96, 96), 96), :]

    def scale_of(first_row, rows):
        row = lax.broadcasted_iota(jnp.int32, (rows, A), 0) + first_row + ni * N
        return jnp.where(row == 0, 0.0, 0.2).astype(F32)

    def source(st):
        def pair(q, _):
            r0 = pl.multiple_of(q * 32, 32)
            p = jnp.concatenate([pert[:, st, pl.ds(r0, 16), :].reshape(192, A),
                                 pert[:, st, pl.ds(pl.multiple_of(r0 + 16, 16), 16), :].reshape(192, A)], axis=1)
            high = p.astype(BF16)
            low = (p - high.astype(F32)).astype(BF16)
            parts = jnp.dot(kc[...], jnp.concatenate([high, low, high], axis=0), preferred_element_type=F32)
            parts = parts.reshape(3, NV, 16, 2 * A)
            p = p.reshape(NV, 16, 2 * A)
            for j in range(2):
                rj = pl.multiple_of(r0 + 16 * j, 16)
                lanes = slice(j * A, (j + 1) * A)
                b5, b6, b7 = (base[f, st, pl.ds(rj, 16), :].astype(F32) for f in (5, 6, 7))
                held = scale_of(rj, 16)
                for v in range(NV):
                    here = p[v, :, lanes]
                    src = parts[0, v, :, lanes] + b5 * parts[1, v, :, lanes] + b6 * parts[2, v, :, lanes] - b7 * here
                    out[v, st, pl.ds(rj, 16), :] = here + (held if 5 <= v <= 9 else 0.2) * src
            return 0
        lax.fori_loop(0, 3, pair, 0, unroll=3)

    def sources(first, count):
        def one(i, _):
            source(i)
            return 0
        lax.fori_loop(first, first + count, one, 0)

    def stream_flux(g):
        for d in (1, 3, 2):
            yf(g, d).wait_recv()
        yown[g].wait()

        def derive(q, _):
            x = jnp.concatenate([yr[g, :, 2 * q].reshape(256, A), yr[g, :, 2 * q + 1].reshape(256, A)], axis=1)
            both = jnp.dot(ks[...], x, preferred_element_type=F32)
            for j in range(2):
                dy[0, 2 * q + j] = both[0:256, j * A:(j + 1) * A]
                dy[1, 2 * q + j] = both[256:512, j * A:(j + 1) * A]
            return 0

        lax.fori_loop(0, NV // 2, derive, 0, unroll=6)

        def mix(q, _):
            dst, pr = q // 2, q % 2
            row = lambda j: pl.multiple_of(dst * 64 + pr * 32 + 16 * j, 16)
            first = jnp.concatenate([dy[0, :, pl.ds(row(j), 16), :].reshape(192, A) for j in range(2)], axis=1)
            low = first.astype(BF16)
            mixed = jnp.dot(ky[...], jnp.concatenate([low, low], axis=0), preferred_element_type=F32)
            mixed = mixed.reshape(NV, 16, 2 * A)
            for j in range(2):
                lanes = slice(j * A, (j + 1) * A)
                near = pl.multiple_of(pr * 32 + 16 * j, 16)
                u, rho, nu = (yr[g, dst, NV + f, pl.ds(near, 16), :].astype(F32) for f in range(3))
                for v in range(NV):
                    d1, d2 = dy[0, v, pl.ds(row(j), 16), :], dy[1, v, pl.ds(row(j), 16), :]
                    flux = nu * d2 - u * d1 - rho * mixed[v, :, lanes]
                    fy[g, dst, v, pl.ds(near, 16), :] = flux.astype(BF16)
            return 0

        lax.fori_loop(0, 8, mix, 0, unroll=2)
        for d in (1, 3, 2):
            yret(g, d).start()

    def azimuth(t, own_blocks, other_blocks, fresh, rows=(0, N // 16)):
        def rows_of(q, _):
            r = pl.ds(pl.multiple_of(q * 16, 16), 16)
            x = [gat[t, slot_own, b, :, r, :].reshape(192, A) for b in own_blocks]
            x += [oth[t, b, :, r, :].reshape(192, A) for b in other_blocks]
            w = [wa[0, b] for b in own_blocks] + [wa[1, b] for b in other_blocks]
            both = lax.dot_general(jnp.concatenate(x, axis=1), jnp.concatenate(w, axis=1), (((1,), (1,)), ((), ())),
                                   preferred_element_type=F32)
            for k in range(2):
                for b in range(4):
                    part = both[:, k * 512 + b * A:k * 512 + (b + 1) * A].reshape(NV, 16, A)
                    if not fresh:
                        part = part + da[t, k, b, :, r, :]
                    da[t, k, b, :, r, :] = part
            return 0

        lax.fori_loop(*rows, rows_of, 0, unroll=3)

    def turned_flux(t, d):
        b = z_of(-d)
        co(t, d).wait_recv()
        for part in range(2):
            cw(t, d, part).wait_recv()
        if d:
            zb(t, d).wait_recv()

        def normal(q, _):
            x = jnp.concatenate([gat[t, :, b, 2 * q].reshape(384, A), gat[t, :, b, 2 * q + 1].reshape(384, A)], axis=1)
            both = jnp.dot(kn[...], x, preferred_element_type=F32)
            for j in range(2):
                for k in range(2):
                    dn[k, 2 * q + j] = both[96 * k:96 * k + 96, j * A:(j + 1) * A]
            return 0

        lax.fori_loop(0, NV // 2, normal, 0, unroll=6)

        def mix(q, _):
            rs = [pl.ds(pl.multiple_of(q * 32 + 16 * j, 16), 16) for j in range(2)]
            low_a = jnp.concatenate([da[t, 0, b, :, r, :].reshape(192, A) for r in rs], axis=1).astype(BF16)
            low_n = jnp.concatenate([dn[0, :, r, :].reshape(192, A) for r in rs], axis=1).astype(BF16)
            mixed = jnp.dot(kz[...], jnp.concatenate([low_a, low_n, low_a, low_n], axis=0), preferred_element_type=F32)
            for j, r in enumerate(rs):
                lanes = slice(j * A, (j + 1) * A)
                u1, u2, rho, nu = (zbase[t, b, f, r, :].astype(F32) for f in range(4))
                for v in range(NV):
                    flux = (nu * (da[t, 1, b, v, r, :] + dn[1, v, r, :]) - u1 * da[t, 0, b, v, r, :] - u2 * dn[0, v, r, :]
                            - rho * mixed[16 * v:16 * v + 16, lanes])
                    fz[t, b, v, r, :] = flux.astype(BF16)
            return 0

        lax.fori_loop(0, N // 32, mix, 0, unroll=3)
        if d:
            zr(t, 4 - d).start()

    def pass_lo(t, d, part):
        if d and not part:
            zf(t, d).wait_recv()
            co(t, d).start()
        lo_c(t, d, part).start()

    def pass_hi(t, d, part):
        lo_c(t, d, part).wait_recv()
        hi_c(t, d, part).start()

    def pass_core(t, d):
        for part in range(2):
            for quarter in (2 * part, 2 * part + 1):
                hi_c(t, d, quarter).wait_recv()
            cw(t, d, part).start()

    def add_stream(g, d):
        i = y_of(-d) * 3 + g
        r = pl.ds(pl.multiple_of(i * 8, 8), 8)
        held = scale_of(i * 8, 8)
        for v in range(NV):
            src = fy[g, y, v] if d == 0 else ry[i, v]
            out[v, :, r, :] += (held if 5 <= v <= 9 else 0.2) * src.astype(F32).reshape(S, 8, A)

    def add_turned(t, d):
        st = 2 * z_of(-d) + t
        held = scale_of(0, N)
        for v in range(NV):
            src = fz[t, z, v] if d == 0 else rz[st, v]
            out[v, st] += (held if 5 <= v <= 9 else 0.2) * src.astype(F32)

    order = [(0, 0, part) for part in range(4)] + [(1, 0, part) for part in [0]]
    order += [(t, d, part) for t in range(2) for d in (1, 3, 2) for part in range(4)]
    order += [(1, 0, part) for part in [1, 2, 3]]

    def step(half):
        for k in (2 * half, 2 * half + 1):
            pass_hi(*order[k])
            if k + 4 < len(order):
                pass_lo(*order[k + 4])

    first, second = (0, N // 32), (N // 32, N // 16)
    sources(0, 2)
    step(0)
    sources(2, 1)
    step(1)
    sources(3, 1)
    step(2)
    sources(4, 1)
    step(3)
    sources(5, 1)
    step(4)
    pass_core(0, 0)
    sources(6, 2)
    step(5)
    step(6)
    stream_flux(0)
    step(7)
    pass_core(0, 1)
    stream_flux(1)
    for w in weights:
        w.wait()
    for c in own:
        c.wait()
    step(8)
    azimuth(0, range(4), range(4), True, first)
    pass_core(0, 3)
    step(9)
    azimuth(0, range(4), range(4), True, second)
    step(10)
    turned_flux(0, 0)
    turned_flux(0, 1)
    pass_core(0, 2)
    step(11)
    turned_flux(0, 3)
    stream_flux(2)
    step(12)
    turned_flux(0, 2)
    pass_core(1, 1)
    azimuth(1, range(4), [z_of(-d) for d in (1, 3)], True, first)
    step(13)
    azimuth(1, range(4), [z_of(-d) for d in (1, 3)], True, second)
    step(14)
    pass_core(1, 3)
    step(15)
    azimuth(1, [], [z_of(-d) for d in (2, 0)], False)
    turned_flux(1, 1)
    turned_flux(1, 3)
    pass_core(1, 2)
    turned_flux(1, 2)
    pass_core(1, 0)
    turned_flux(1, 0)
    for g in range(3):
        add_stream(g, 0)
        for d in (1, 3, 2):
            yret(g, d).wait_recv()
            add_stream(g, d)
    for t in range(2):
        for d in (0, 1, 3, 2):
            if d:
                zr(t, d).wait_recv()
            add_turned(t, d)
    for t in range(2):
        for d in range(4):
            co(t, d).wait_send()
            for part in range(2):
                cw(t, d, part).wait_send()
            for part in range(PARTS):
                lo_c(t, d, part).wait_send()
                hi_c(t, d, part).wait_send()
        for d in (1, 2, 3):
            for copy in (zf, zb, zr):
                copy(t, d).wait_send()
    for g in range(3):
        for d in (1, 2, 3):
            yf(g, d).wait_send()
            yret(g, d).wait_send()


def shards(perturbation, base_flow, stream_ops, azimuth_ops, normal_ops, coupling, chemistry):
    vmem = pl.BlockSpec(memory_space=pltpu.VMEM)
    hbm = pl.BlockSpec(memory_space=pl.ANY)
    scratch = lambda *shape: pltpu.VMEM(shape, BF16)
    return pl.pallas_call(
        kernel,
        out_shape=pltpu.VMEM(perturbation.shape, F32),
        in_specs=[hbm] * 7,
        out_specs=vmem,
        scratch_shapes=[
            pltpu.VMEM((NV, S, N, A), F32),
            scratch(8, S, N, A),
            scratch(2, 32, 32),
            scratch(2, 384, 384),
            pltpu.VMEM((3, NV, NV), F32),
            pltpu.VMEM((3, NV, NV), F32),
            scratch(S, NV, N, A),
            scratch(S, 4, N, A),
            scratch(2, 4, 4, NV, N, A),
            scratch(2, 4, 4, N, A),
            scratch(2, 4, NV, N, A),
            scratch(12, 15, 64, A),
            scratch(3, 4, 15, 64, A),
            scratch(3, 4, NV, 64, A),
            scratch(12, NV, 64, A),
            scratch(2, 4, NV, N, A),
            scratch(S, NV, N, A),
            pltpu.VMEM((2, 2, 4, NV, N, A), F32),
            pltpu.VMEM((2, NV, N, A), F32),
            pltpu.VMEM((2, NV, 256, A), F32),
            scratch(2, 4, 1024, A),
            scratch(576, 576),
            scratch(192, 384),
            scratch(192, 768),
            scratch(512, 256),
            scratch(192, 384),
            pltpu.SemaphoreType.DMA((COPIES,)),
            pltpu.SemaphoreType.DMA((COPIES,)),
            pltpu.SemaphoreType.DMA((11,)),
            pltpu.SemaphoreType.DMA((2 * S + 4,)),
            pltpu.SemaphoreType.DMA((16,)),
        ],
        compiler_params=pltpu.CompilerParams(collective_id=0, has_side_effects=True, vmem_limit_bytes=56 << 20),
    )(perturbation, base_flow, stream_ops, azimuth_ops, normal_ops, coupling, chemistry)


def solution(mesh):
    field = P(None, "stream", "normal", "azim")
    return jax.shard_map(
        shards,
        mesh=mesh,
        in_specs=(field, field, P(), P(), P(), P(), P()),
        out_specs=field,
        check_vma=False,
    )
```

```python
import functools

import jax
import jax.numpy as jnp
from jax import lax
from jax.experimental import pallas as pl
from jax.experimental.pallas import tpu as pltpu
from jax.sharding import PartitionSpec as P

MESH = pl.DeviceIdType.MESH
F32, BF16 = jnp.float32, jnp.bfloat16
NV, S, N, A = 12, 8, 96, 128


PARTS = 4


def copies_table():
    table, count = {}, 0
    for t in range(2):
        for d in (1, 2, 3):
            for name in ("zf", "zb", "zr"):
                table[name, t, d] = count
                count += 1
        for d in range(4):
            table["co", t, d] = count
            count += 1
            for part in range(2):
                table["cw", t, d, part] = count
                count += 1
            for part in range(PARTS):
                for name in ("lo", "hi"):
                    table[name, t, d, part] = count
                    count += 1
    for g in range(3):
        for d in (1, 2, 3):
            for name in ("yf", "yr"):
                table[name, g, d] = count
                count += 1
    return table, count


TABLE, COPIES = copies_table()


def spread(matrix, reps):
    rows, cols = matrix.shape
    shift = reps.bit_length() - 1
    up = (lax.broadcasted_iota(jnp.int32, (rows * reps, rows), 0) >> shift
          == lax.broadcasted_iota(jnp.int32, (rows * reps, rows), 1)).astype(F32).astype(BF16)
    wide = (lax.broadcasted_iota(jnp.int32, (cols, cols * reps), 1) >> shift
            == lax.broadcasted_iota(jnp.int32, (cols, cols * reps), 0)).astype(F32).astype(BF16)
    tall = jnp.dot(up, matrix, preferred_element_type=F32).astype(BF16)
    full = jnp.dot(tall, wide, preferred_element_type=F32)
    r = lax.broadcasted_iota(jnp.int32, full.shape, 0) & (reps - 1)
    c = lax.broadcasted_iota(jnp.int32, full.shape, 1) & (reps - 1)
    return jnp.where(r == c, full, 0.0).astype(BF16)


def split_two(matrix):
    high = matrix.astype(BF16)
    return high, (matrix - high.astype(F32)).astype(BF16)


def kernel(pert_hbm, base_hbm, sops_hbm, aops, nops_hbm, coup_hbm, chem_hbm, out,
           pert, base, sops, nops, coup, chem, zs, zbs, gat, zbase, oth, ys, yr, fy, ry, fz, rz, da, dn, dy, wa, kc, ky, kz, ks, kn,
           ssem, rsem, lsem, isem, wsem):
    y = lax.axis_index("stream")
    ai = lax.axis_index("azim")
    ni = lax.axis_index("normal")
    lo, z = ai // 4, ai % 4
    hi, core = ni // 2, ni % 2

    def at(y_=None, z_=None, lo_=None, hi_=None, core_=None):
        pick = lambda new, old: old if new is None else new
        return {"stream": pick(y_, y), "azim": pick(lo_, lo) * 4 + pick(z_, z),
                "normal": pick(hi_, hi) * 2 + pick(core_, core)}

    y_of = lambda d: (y + d) % 4
    z_of = lambda d: (z + d) % 4
    lo_dev = at(lo_=1 - lo)
    hi_dev = at(lo_=1 - lo, hi_=1 - hi)
    core_dev = at(core_=1 - core)
    slot_own = ni
    slot_core = hi * 2 + (1 - core)
    slot_hi = (1 - hi) * 2 + core
    slot_both = (1 - hi) * 2 + (1 - core)

    stations = [2 * z_of(d) + t for t in range(2) for d in (0, 1, 3, 2)]
    loads = [(pltpu.make_async_copy(pert_hbm.at[:, st], pert.at[:, st], isem.at[2 * i]),
              pltpu.make_async_copy(base_hbm.at[:, st], base.at[:, st], isem.at[2 * i + 1]))
             for i, st in enumerate(stations)]
    for pair in loads:
        for load in pair:
            load.start()
    small = [pltpu.make_async_copy(far, near, isem.at[2 * S + i]) for i, (far, near) in enumerate(
        ((sops_hbm, sops), (nops_hbm, nops), (coup_hbm, coup), (chem_hbm, chem)))]
    for load in small:
        load.start()
    barrier = pltpu.get_barrier_semaphore()
    partners = [at(y_=y_of(d)) for d in (1, 2, 3)] + [at(z_=z_of(d)) for d in (1, 2, 3)] + [lo_dev, hi_dev, core_dev]
    for device in partners:
        pl.semaphore_signal(barrier, inc=1, device_id=device, device_id_type=MESH)

    def remote(src, dst, key, device):
        i = TABLE[key]
        return pltpu.make_async_remote_copy(src_ref=src, dst_ref=dst, send_sem=ssem.at[i], recv_sem=rsem.at[i],
                                            device_id=device, device_id_type=MESH)

    def zf(t, d):
        return remote(zs.at[2 * z_of(d) + t], gat.at[t, slot_own, z], ("zf", t, d), at(z_=z_of(d)))

    def zb(t, d):
        return remote(zbs.at[2 * z_of(d) + t], zbase.at[t, z], ("zb", t, d), at(z_=z_of(d)))

    def zr(t, d):
        return remote(fz.at[t, z_of(d)], rz.at[2 * z + t], ("zr", t, d), at(z_=z_of(d)))

    def src_own(t, d):
        return zs.at[2 * z + t] if d == 0 else gat.at[t, slot_own, z_of(-d)]

    def piece(ref, part, parts=PARTS):
        return ref.at[pl.ds(part * (NV // parts), NV // parts)]

    def lo_c(t, d, part):
        return remote(piece(src_own(t, d), part), piece(oth.at[t, z_of(-d)], part), ("lo", t, d, part), lo_dev)

    def co(t, d):
        return remote(src_own(t, d), gat.at[t, slot_own, z_of(-d)], ("co", t, d), core_dev)

    def hi_c(t, d, part):
        return remote(piece(oth.at[t, z_of(-d)], part), piece(gat.at[t, slot_own, z_of(-d)], part), ("hi", t, d, part), hi_dev)

    def cw(t, d, part):
        here = piece(gat.at[t, slot_hi, z_of(-d)], part, 2)
        return remote(here, here, ("cw", t, d, part), core_dev)

    def yf(g, d):
        return remote(ys.at[y_of(d) * 3 + g], yr.at[g, y], ("yf", g, d), at(y_=y_of(d)))

    def yret(g, d):
        return remote(fy.at[g, y_of(d)], ry.at[y * 3 + g], ("yr", g, d), at(y_=y_of(d)))

    def lower(i):
        for load in loads[i]:
            load.wait()
        st = stations[i]
        zs[st] = pert[:, st].astype(BF16)
        for f in range(4):
            zbs[st, f] = base[1 + f, st]

    lower(0)
    pl.semaphore_wait(barrier, len(partners))
    for part in range(PARTS):
        lo_c(0, 0, part).start()
    co(0, 0).start()
    for i, d in enumerate((1, 3, 2)):
        lower(1 + i)
        zf(0, d).start()
    lower(4)
    co(1, 0).start()
    for i in (5, 6, 7):
        lower(i)
    own = []
    for t in range(2):
        own.append(pltpu.make_async_copy(zs.at[2 * z + t], gat.at[t, slot_own, z], lsem.at[4 + t]))
        own.append(pltpu.make_async_copy(zbs.at[2 * z + t], zbase.at[t, z], lsem.at[6 + t]))
    for c in own:
        c.start()

    def lower_y(i, _):
        rows = pert[:, :, pl.ds(pl.multiple_of(i * 8, 8), 8), :]
        ys[i, 0:NV] = rows.reshape(NV, 64, A).astype(BF16)
        return 0

    lax.fori_loop(0, 12, lower_y, 0)
    for j, f in enumerate((0, 3, 4)):
        wide = base[f].astype(F32)
        for i in range(12):
            ys[i, NV + j] = wide[:, 8 * i:8 * i + 8, :].reshape(64, A).astype(BF16)
    for g in range(3):
        for d in (1, 3, 2):
            yf(g, d).start()
    for d in (1, 3, 2):
        zf(1, d).start()
    for t in range(2):
        for d in (1, 3, 2):
            zb(t, d).start()
    yown = []
    for g in range(3):
        yown.append(pltpu.make_async_copy(ys.at[y * 3 + g], yr.at[g, y], lsem.at[8 + g]))
    for c in yown:
        c.start()
    weights = [
        pltpu.make_async_copy(
            aops.at[k, pl.ds(pl.multiple_of(lo * 512, 512), 512), pl.ds(pl.multiple_of(half * 512 + b * A, A), A)],
            wa.at[j, b, pl.ds(k * 512, 512)], wsem.at[8 * k + 4 * j + b])
        for k in range(2) for j, half in enumerate((lo, 1 - lo)) for b in range(4)
    ]
    for w in weights:
        w.start()

    for load in small:
        load.wait()
    ks[...] = spread(sops[...].reshape(64, 32), 8)
    c_high, c_low = split_two(coup[...])
    ky[:, 0:192] = spread(c_high[0], 16)
    ky[:, 192:384] = spread(c_low[0], 16)
    kz[:, 0:192] = spread(c_high[1], 16)
    kz[:, 192:384] = spread(c_high[2], 16)
    kz[:, 384:576] = spread(c_low[1], 16)
    kz[:, 576:768] = spread(c_low[2], 16)
    h_high, h_low = split_two(chem[...])
    for c in range(3):
        high = spread(h_high[c], 16)
        kc[192 * c:192 * c + 192, 0:192] = high
        kc[192 * c:192 * c + 192, 192:384] = high
        kc[192 * c:192 * c + 192, 384:576] = spread(h_low[c], 16)
    for k in range(2):
        kn[96 * k:96 * k + 96] = nops[k, pl.ds(pl.multiple_of(ni * 96, 96), 96), :]

    def scale_of(first_row, rows):
        row = lax.broadcasted_iota(jnp.int32, (rows, A), 0) + first_row + ni * N
        return jnp.where(row == 0, 0.0, 0.2).astype(F32)

    def source(st):
        def pair(q, _):
            r0 = pl.multiple_of(q * 32, 32)
            p = jnp.concatenate([pert[:, st, pl.ds(r0, 16), :].reshape(192, A),
                                 pert[:, st, pl.ds(pl.multiple_of(r0 + 16, 16), 16), :].reshape(192, A)], axis=1)
            high = p.astype(BF16)
            low = (p - high.astype(F32)).astype(BF16)
            parts = jnp.dot(kc[...], jnp.concatenate([high, low, high], axis=0), preferred_element_type=F32)
            parts = parts.reshape(3, NV, 16, 2 * A)
            p = p.reshape(NV, 16, 2 * A)
            for j in range(2):
                rj = pl.multiple_of(r0 + 16 * j, 16)
                lanes = slice(j * A, (j + 1) * A)
                b5, b6, b7 = (base[f, st, pl.ds(rj, 16), :].astype(F32) for f in (5, 6, 7))
                held = scale_of(rj, 16)
                for v in range(NV):
                    here = p[v, :, lanes]
                    src = parts[0, v, :, lanes] + b5 * parts[1, v, :, lanes] + b6 * parts[2, v, :, lanes] - b7 * here
                    out[v, st, pl.ds(rj, 16), :] = here + (held if 5 <= v <= 9 else 0.2) * src
            return 0
        lax.fori_loop(0, 3, pair, 0, unroll=3)

    def sources(first, count):
        def one(i, _):
            source(i)
            return 0
        lax.fori_loop(first, first + count, one, 0)

    def stream_flux(g):
        for d in (1, 3, 2):
            yf(g, d).wait_recv()
        yown[g].wait()

        def derive(q, _):
            x = jnp.concatenate([yr[g, :, 2 * q].reshape(256, A), yr[g, :, 2 * q + 1].reshape(256, A)], axis=1)
            both = jnp.dot(ks[...], x, preferred_element_type=F32)
            for j in range(2):
                dy[0, 2 * q + j] = both[0:256, j * A:(j + 1) * A]
                dy[1, 2 * q + j] = both[256:512, j * A:(j + 1) * A]
            return 0

        lax.fori_loop(0, NV // 2, derive, 0, unroll=6)

        def mix(q, _):
            dst, pr = q // 2, q % 2
            row = lambda j: pl.multiple_of(dst * 64 + pr * 32 + 16 * j, 16)
            first = jnp.concatenate([dy[0, :, pl.ds(row(j), 16), :].reshape(192, A) for j in range(2)], axis=1)
            low = first.astype(BF16)
            mixed = jnp.dot(ky[...], jnp.concatenate([low, low], axis=0), preferred_element_type=F32)
            mixed = mixed.reshape(NV, 16, 2 * A)
            for j in range(2):
                lanes = slice(j * A, (j + 1) * A)
                near = pl.multiple_of(pr * 32 + 16 * j, 16)
                u, rho, nu = (yr[g, dst, NV + f, pl.ds(near, 16), :].astype(F32) for f in range(3))
                for v in range(NV):
                    d1, d2 = dy[0, v, pl.ds(row(j), 16), :], dy[1, v, pl.ds(row(j), 16), :]
                    flux = nu * d2 - u * d1 - rho * mixed[v, :, lanes]
                    fy[g, dst, v, pl.ds(near, 16), :] = flux.astype(BF16)
            return 0

        lax.fori_loop(0, 8, mix, 0, unroll=2)
        for d in (1, 3, 2):
            yret(g, d).start()

    def azimuth(t, own_blocks, other_blocks, fresh, rows=(0, N // 16)):
        def rows_of(q, _):
            r = pl.ds(pl.multiple_of(q * 16, 16), 16)
            x = [gat[t, slot_own, b, :, r, :].reshape(192, A) for b in own_blocks]
            x += [oth[t, b, :, r, :].reshape(192, A) for b in other_blocks]
            w = [wa[0, b] for b in own_blocks] + [wa[1, b] for b in other_blocks]
            both = lax.dot_general(jnp.concatenate(x, axis=1), jnp.concatenate(w, axis=1), (((1,), (1,)), ((), ())),
                                   preferred_element_type=F32)
            for k in range(2):
                for b in range(4):
                    part = both[:, k * 512 + b * A:k * 512 + (b + 1) * A].reshape(NV, 16, A)
                    if not fresh:
                        part = part + da[t, k, b, :, r, :]
                    da[t, k, b, :, r, :] = part
            return 0

        lax.fori_loop(*rows, rows_of, 0, unroll=3)

    def turned_flux(t, d):
        b = z_of(-d)
        co(t, d).wait_recv()
        for part in range(2):
            cw(t, d, part).wait_recv()
        if d:
            zb(t, d).wait_recv()

        def normal(q, _):
            x = jnp.concatenate([gat[t, :, b, 2 * q].reshape(384, A), gat[t, :, b, 2 * q + 1].reshape(384, A)], axis=1)
            both = jnp.dot(kn[...], x, preferred_element_type=F32)
            for j in range(2):
                for k in range(2):
                    dn[k, 2 * q + j] = both[96 * k:96 * k + 96, j * A:(j + 1) * A]
            return 0

        lax.fori_loop(0, NV // 2, normal, 0, unroll=6)

        def mix(q, _):
            rs = [pl.ds(pl.multiple_of(q * 32 + 16 * j, 16), 16) for j in range(2)]
            low_a = jnp.concatenate([da[t, 0, b, :, r, :].reshape(192, A) for r in rs], axis=1).astype(BF16)
            low_n = jnp.concatenate([dn[0, :, r, :].reshape(192, A) for r in rs], axis=1).astype(BF16)
            mixed = jnp.dot(kz[...], jnp.concatenate([low_a, low_n, low_a, low_n], axis=0), preferred_element_type=F32)
            for j, r in enumerate(rs):
                lanes = slice(j * A, (j + 1) * A)
                u1, u2, rho, nu = (zbase[t, b, f, r, :].astype(F32) for f in range(4))
                for v in range(NV):
                    flux = (nu * (da[t, 1, b, v, r, :] + dn[1, v, r, :]) - u1 * da[t, 0, b, v, r, :] - u2 * dn[0, v, r, :]
                            - rho * mixed[16 * v:16 * v + 16, lanes])
                    fz[t, b, v, r, :] = flux.astype(BF16)
            return 0

        lax.fori_loop(0, N // 32, mix, 0, unroll=3)
        if d:
            zr(t, 4 - d).start()

    def pass_lo(t, d, part):
        if d and not part:
            zf(t, d).wait_recv()
            co(t, d).start()
        lo_c(t, d, part).start()

    def pass_hi(t, d, part):
        lo_c(t, d, part).wait_recv()
        hi_c(t, d, part).start()

    def pass_core(t, d):
        for part in range(2):
            for quarter in (2 * part, 2 * part + 1):
                hi_c(t, d, quarter).wait_recv()
            cw(t, d, part).start()

    def add_stream(g, d):
        i = y_of(-d) * 3 + g
        r = pl.ds(pl.multiple_of(i * 8, 8), 8)
        held = scale_of(i * 8, 8)
        for v in range(NV):
            src = fy[g, y, v] if d == 0 else ry[i, v]
            out[v, :, r, :] += (held if 5 <= v <= 9 else 0.2) * src.astype(F32).reshape(S, 8, A)

    def add_turned(t, d):
        st = 2 * z_of(-d) + t
        held = scale_of(0, N)
        for v in range(NV):
            src = fz[t, z, v] if d == 0 else rz[st, v]
            out[v, st] += (held if 5 <= v <= 9 else 0.2) * src.astype(F32)

    order = [(0, 0, part) for part in range(4)] + [(1, 0, part) for part in [0]]
    order += [(t, d, part) for t in range(2) for d in (1, 3, 2) for part in range(4)]
    order += [(1, 0, part) for part in [1, 2, 3]]

    def step(half):
        for k in (2 * half, 2 * half + 1):
            pass_hi(*order[k])
            if k + 4 < len(order):
                pass_lo(*order[k + 4])

    first, second = (0, N // 32), (N // 32, N // 16)
    sources(0, 2)
    step(0)
    sources(2, 1)
    step(1)
    sources(3, 1)
    step(2)
    sources(4, 1)
    step(3)
    sources(5, 1)
    step(4)
    pass_core(0, 0)
    sources(6, 2)
    step(5)
    step(6)
    stream_flux(0)
    step(7)
    pass_core(0, 1)
    stream_flux(1)
    for w in weights:
        w.wait()
    for c in own:
        c.wait()
    step(8)
    azimuth(0, range(4), range(4), True, first)
    pass_core(0, 3)
    step(9)
    azimuth(0, range(4), range(4), True, second)
    step(10)
    turned_flux(0, 0)
    turned_flux(0, 1)
    pass_core(0, 2)
    step(11)
    turned_flux(0, 3)
    stream_flux(2)
    step(12)
    turned_flux(0, 2)
    pass_core(1, 1)
    azimuth(1, range(4), [z_of(-d) for d in (1, 3)], True, first)
    step(13)
    azimuth(1, range(4), [z_of(-d) for d in (1, 3)], True, second)
    step(14)
    pass_core(1, 3)
    azimuth(1, [], [z_of(-2)], False)
    step(15)
    azimuth(1, [], [z], False)
    turned_flux(1, 1)
    turned_flux(1, 3)
    pass_core(1, 2)
    turned_flux(1, 2)
    pass_core(1, 0)
    turned_flux(1, 0)
    for g in range(3):
        add_stream(g, 0)
        for d in (1, 3, 2):
            yret(g, d).wait_recv()
            add_stream(g, d)
    for t in range(2):
        for d in (0, 1, 3, 2):
            if d:
                zr(t, d).wait_recv()
            add_turned(t, d)
    for t in range(2):
        for d in range(4):
            co(t, d).wait_send()
            for part in range(2):
                cw(t, d, part).wait_send()
            for part in range(PARTS):
                lo_c(t, d, part).wait_send()
                hi_c(t, d, part).wait_send()
        for d in (1, 2, 3):
            for copy in (zf, zb, zr):
                copy(t, d).wait_send()
    for g in range(3):
        for d in (1, 2, 3):
            yf(g, d).wait_send()
            yret(g, d).wait_send()


def shards(perturbation, base_flow, stream_ops, azimuth_ops, normal_ops, coupling, chemistry):
    vmem = pl.BlockSpec(memory_space=pltpu.VMEM)
    hbm = pl.BlockSpec(memory_space=pl.ANY)
    scratch = lambda *shape: pltpu.VMEM(shape, BF16)
    return pl.pallas_call(
        kernel,
        out_shape=pltpu.VMEM(perturbation.shape, F32),
        in_specs=[hbm] * 7,
        out_specs=vmem,
        scratch_shapes=[
            pltpu.VMEM((NV, S, N, A), F32),
            scratch(8, S, N, A),
            scratch(2, 32, 32),
            scratch(2, 384, 384),
            pltpu.VMEM((3, NV, NV), F32),
            pltpu.VMEM((3, NV, NV), F32),
            scratch(S, NV, N, A),
            scratch(S, 4, N, A),
            scratch(2, 4, 4, NV, N, A),
            scratch(2, 4, 4, N, A),
            scratch(2, 4, NV, N, A),
            scratch(12, 15, 64, A),
            scratch(3, 4, 15, 64, A),
            scratch(3, 4, NV, 64, A),
            scratch(12, NV, 64, A),
            scratch(2, 4, NV, N, A),
            scratch(S, NV, N, A),
            pltpu.VMEM((2, 2, 4, NV, N, A), F32),
            pltpu.VMEM((2, NV, N, A), F32),
            pltpu.VMEM((2, NV, 256, A), F32),
            scratch(2, 4, 1024, A),
            scratch(576, 576),
            scratch(192, 384),
            scratch(192, 768),
            scratch(512, 256),
            scratch(192, 384),
            pltpu.SemaphoreType.DMA((COPIES,)),
            pltpu.SemaphoreType.DMA((COPIES,)),
            pltpu.SemaphoreType.DMA((11,)),
            pltpu.SemaphoreType.DMA((2 * S + 4,)),
            pltpu.SemaphoreType.DMA((16,)),
        ],
        compiler_params=pltpu.CompilerParams(collective_id=0, has_side_effects=True, vmem_limit_bytes=56 << 20),
    )(perturbation, base_flow, stream_ops, azimuth_ops, normal_ops, coupling, chemistry)


def solution(mesh):
    field = P(None, "stream", "normal", "azim")
    return jax.shard_map(
        shards,
        mesh=mesh,
        in_specs=(field, field, P(), P(), P(), P(), P()),
        out_specs=field,
        check_vma=False,
    )
```
